512 devices in a mesh: dp: 32 (over x, z), table: 16 (over y, core).
Axes of the slice: x: 4, y: 8, z: 8, core: 2. Of those that a mesh axis runs over, the one named last changes fastest.
Arguments:
- dense_feats: bfloat16 [65536, 13], P(('dp', 'table')), may hold values from -6 to 6
- lookup_ids: int32 [32, 8, 65536], P('table', None, 'dp'), may hold values from 0 to 2047
- lookup_counts: int32 [32, 65536], P('table', 'dp'), may hold values from 0 to 8
- shard_table: int32 [32], replicated, may hold values from 0 to 25, as said below
- embed_tables: bfloat16 [32, 2048, 128], P('table'), may hold values from -6 to 6
- first_layer: bfloat16 [13, 512], replicated, may hold values from -1.75 to 1.75
- first_offset: float32 [512], replicated, may hold values from -3 to 3
- second_layer: bfloat16 [512, 256], replicated, may hold values from -0.25 to 0.25
- second_offset: float32 [256], replicated, may hold values from -3 to 3
- third_layer: bfloat16 [256, 128], replicated, may hold values from -0.375 to 0.375
- third_offset: float32 [128], replicated, may hold values from -3 to 3
- cross_down: bfloat16 [3456, 512], P(None, 'table'), may hold values from -0.109375 to 0.109375
- cross_up: bfloat16 [512, 3456], P('table'), may hold values from -0.25 to 0.25
- cross_bias: float32 [3456], replicated, may hold values from -3 to 3
- cotangent: bfloat16 [65536, 3456], P(('dp', 'table')), may hold values from -0.059814453 to 0.059814453
Outputs:
- table_grad: float32 [32, 2048, 128], P('table', 'dp')
- first_layer_grad: float32 [13, 512], replicated
- first_offset_grad: float32 [512], replicated
- second_layer_grad: float32 [512, 256], replicated
- second_offset_grad: float32 [256], replicated
- third_layer_grad: float32 [256, 128], replicated
- third_offset_grad: float32 [128], replicated
- cross_bias_grad: float32 [3456], replicated
The draws below stay inside these ranges and needn't reach their ends.
Inputs may be any that keep to these rules, and one draw needn't show every extreme that they name: `shard_table`: every table has at least one shard.
All inputs are finite; a program needn't handle non-finite values.
Results may differ from the reference program's by a relative error of at most 0.0085.
Values may be sent and summed in bfloat16 or wider, within the bound.
No kernel may reach another device: no remote copies, remote signals or barrier semaphores. Data moves between devices by JAX's collectives and lax.ppermute only.
A program may use at most 64 MiB of HBM per device.

```python
import math
import jax
import jax.numpy as jnp
import numpy as np
from jax import lax

TABLES = 26
EMB = 128
DENSE = 13
H1 = 512
H2 = 256
RANK = 512
SHARDS = 32
HOT = 8
ROWS = 2048
EX_DEV = 128
CROSS_IN = 3456
BATCH = 65536
N_DP = 32
N_TABLE = 16


def draw_shard_table(key, part):
    first_key, second_key = jax.random.split(jax.random.fold_in(key, 17))
    extra = jax.random.randint(first_key, (SHARDS - TABLES,), 0, TABLES).astype(jnp.int32)
    base = jnp.concatenate([jnp.arange(TABLES, dtype=jnp.int32), extra])
    order = jax.random.permutation(second_key, SHARDS)
    return base[order]


def touch_ends(drawn, key, smallest, largest):
    place = [jax.random.randint(jax.random.fold_in(key, axis), (), 0, length) for axis, length in enumerate(drawn.shape)]
    widest = drawn.shape.index(max(drawn.shape))
    neighbour = place[:widest] + [(place[widest] + 1) % drawn.shape[widest]] + place[widest + 1:]
    return drawn.at[tuple(place)].set(smallest).at[tuple(neighbour)].set(largest)


def block_scale(rng, dims, shards, low, high):
    level = 1.0
    for position, blocks in shards:
        steps = jax.random.uniform(jax.random.fold_in(jax.random.fold_in(rng, 6), position), (blocks,), jnp.float32, low / len(shards), high / len(shards))
        level = level * jnp.repeat(jnp.exp(steps), dims[position] // blocks).reshape((-1,) + (1,) * (len(dims) - 1 - position))
    return level


def rank_table(number_of, slope):
    loads = [(1 << 20) // math.isqrt(rank ** slope) + 1 for rank in range(1, number_of + 1)]
    scale = 1 + sum(loads) // (1 << 30)
    return np.cumsum(np.array([max(1, weight // scale) for weight in loads]))


def skewed_ids(rng, shape, number_of, slope):
    listing = rank_table(number_of, slope)
    lot = jax.random.randint(jax.random.fold_in(rng, 1), shape, 0, int(listing[number_of - 1]))
    standing = jnp.searchsorted(jnp.asarray(listing, jnp.int32), lot, side="right")
    return jax.random.permutation(jax.random.fold_in(rng, 2), number_of)[standing].astype(jnp.int32)


def normal_values(stream_key, shape, deviation, most, cuts=(), kind=jnp.bfloat16):
    values = jax.random.normal(stream_key, shape, jnp.float32) * deviation
    if len(cuts) > 0:
        values = block_scale(stream_key, shape, cuts, -0.22, 0.18) * values
    return jnp.clip(values, min=-most, max=most).astype(kind)


def setup_inputs(seed: int = 0) -> dict:
    splits = jax.random.split(jax.random.key(seed), 16)
    dense_feats = normal_values(splits[0], (BATCH, DENSE), 1.0, 6.0, ((0, 512),))
    lookup_ids = touch_ends(skewed_ids(splits[1], (SHARDS, HOT, BATCH), ROWS, 2), jax.random.fold_in(splits[1], 3), 0, ROWS - 1).astype(jnp.int32)
    lookup_counts = touch_ends(jax.random.randint(splits[2], (SHARDS, BATCH), 0, HOT + 1), jax.random.fold_in(splits[2], 1), 0, HOT).astype(jnp.int32)
    shard_table = draw_shard_table(jax.random.fold_in(splits[15], 71), 0)
    embed_tables = normal_values(splits[4], (SHARDS, ROWS, EMB), 1.0, 6.0, ((0, 16),))
    first_layer = normal_values(splits[5], (DENSE, H1), DENSE ** -0.5, 1.75)
    first_offset = normal_values(splits[6], (H1,), 0.5, 3.0, (), jnp.float32)
    second_layer = normal_values(splits[7], (H1, H2), H1 ** -0.5, 0.25)
    second_offset = normal_values(splits[8], (H2,), 0.5, 3.0, (), jnp.float32)
    third_layer = normal_values(splits[9], (H2, EMB), H2 ** -0.5, 0.375)
    third_offset = normal_values(splits[10], (EMB,), 0.5, 3.0, (), jnp.float32)
    cross_down = normal_values(splits[11], (CROSS_IN, RANK), CROSS_IN ** -0.5, 0.109375, ((1, 16),))
    cross_up = normal_values(splits[12], (RANK, CROSS_IN), RANK ** -0.5, 0.25, ((0, 16),))
    cross_bias = normal_values(splits[13], (CROSS_IN,), 0.5, 3.0, (), jnp.float32)
    cotangent = normal_values(splits[14], (BATCH, CROSS_IN), 0.01, 0.059814453, ((0, 512),))
    return {"dense_feats": dense_feats, "lookup_ids": lookup_ids, "lookup_counts": lookup_counts, "shard_table": shard_table, "embed_tables": embed_tables, "first_layer": first_layer, "first_offset": first_offset, "second_layer": second_layer, "second_offset": second_offset, "third_layer": third_layer, "third_offset": third_offset, "cross_down": cross_down, "cross_up": cross_up, "cross_bias": cross_bias, "cotangent": cotangent}


def silu_slope(value):
    sigmoid = 1.0 / (1.0 + jnp.exp(-value))
    return sigmoid * (1.0 + value * (1.0 - sigmoid))


def bottom_pass(dense_rows, first_layer, first_offset, second_layer, second_offset, third_layer, third_offset):
    first_pre = jnp.dot(dense_rows, first_layer, preferred_element_type=jnp.float32) + first_offset.astype(jnp.float32)
    first_act = jax.nn.silu(first_pre).astype(jnp.bfloat16)
    second_pre = jnp.dot(first_act, second_layer, preferred_element_type=jnp.float32) + second_offset.astype(jnp.float32)
    second_act = jax.nn.silu(second_pre).astype(jnp.bfloat16)
    third_pre = jnp.dot(second_act, third_layer, preferred_element_type=jnp.float32) + third_offset.astype(jnp.float32)
    bottom_out = jax.nn.silu(third_pre).astype(jnp.bfloat16)
    return bottom_out, (first_pre, first_act, second_pre, second_act, third_pre)


def bottom_back(dense_rows, saved, second_layer, third_layer, bottom_grad):
    first_pre, first_act, second_pre, second_act, third_pre = saved
    contract = (((0,), (0,)), ((), ()))
    back_dims = (((1,), (1,)), ((), ()))
    third_delta = (silu_slope(third_pre) * bottom_grad.astype(jnp.float32)).astype(jnp.bfloat16)
    third_grad = lax.dot_general(second_act, third_delta, contract, preferred_element_type=jnp.float32)
    third_bias = jnp.sum(third_delta.astype(jnp.float32), axis=0)
    second_back = lax.dot_general(third_delta, third_layer, back_dims, preferred_element_type=jnp.float32)
    second_delta = (silu_slope(second_pre) * second_back).astype(jnp.bfloat16)
    second_grad = lax.dot_general(first_act, second_delta, contract, preferred_element_type=jnp.float32)
    second_bias = jnp.sum(second_delta.astype(jnp.float32), axis=0)
    first_back = lax.dot_general(second_delta, second_layer, back_dims, preferred_element_type=jnp.float32)
    first_delta = (silu_slope(first_pre) * first_back).astype(jnp.bfloat16)
    first_grad = lax.dot_general(dense_rows, first_delta, contract, preferred_element_type=jnp.float32)
    first_bias = jnp.sum(first_delta.astype(jnp.float32), axis=0)
    parts = (first_grad, first_bias, second_grad, second_bias, third_grad, third_bias)
    return tuple(piece.astype(jnp.float32) for piece in parts)


def zeros_float(shape):
    return jnp.zeros(shape, dtype=jnp.float32)


def reference(dense_feats, lookup_ids, lookup_counts, shard_table, embed_tables, first_layer, first_offset, second_layer, second_offset, third_layer, third_offset, cross_down, cross_up, cross_bias, cotangent):
    group = EX_DEV * N_TABLE
    table_onehot = (shard_table[:, None] == jnp.arange(TABLES, dtype=jnp.int32)[None, :]).astype(jnp.float32)
    slot_iota = jnp.arange(HOT, dtype=jnp.int32)
    back_dims = (((1,), (1,)), ((), ()))

    def pool_one(inputs):
        table_rows, index_rows, count_rows = inputs
        picked = jnp.take(table_rows.astype(jnp.float32), index_rows.astype(jnp.int32), axis=0)
        valid = (count_rows[None, :] > slot_iota[:, None]).astype(jnp.float32)
        return jnp.sum(picked * valid[:, :, None], axis=0).astype(jnp.bfloat16)

    def grad_one(inputs):
        index_rows, count_rows, grad_rows = inputs
        valid = (count_rows[None, :] > slot_iota[:, None]).astype(jnp.float32)
        contrib = valid[:, :, None] * grad_rows.astype(jnp.float32)[None, :, :]
        summed = jax.ops.segment_sum(contrib.reshape(-1, EMB), index_rows.reshape(-1).astype(jnp.int32), num_segments=ROWS)
        return summed.astype(jnp.float32)

    def block_step(running, block_number):
        start = (block_number * group).astype(jnp.int32)
        index_block = lax.dynamic_slice_in_dim(lookup_ids, start, group, 2)
        count_block = lax.dynamic_slice_in_dim(lookup_counts, start, group, 1)
        dense_rows = lax.dynamic_slice_in_dim(dense_feats, start, group, 0)
        cot_rows = lax.dynamic_slice_in_dim(cotangent, start, group, 0)
        pooled = lax.map(pool_one, (embed_tables, index_block, count_block))
        table_pooled = jnp.einsum("sbe,st->bte", pooled.astype(jnp.float32), table_onehot).astype(jnp.bfloat16)
        bottom_out, saved = bottom_pass(dense_rows, first_layer, first_offset, second_layer, second_offset, third_layer, third_offset)
        cross_input = jnp.concatenate([bottom_out[:, None, :], table_pooled], axis=1).reshape(group, CROSS_IN)
        low_rank = jnp.dot(cross_input, cross_down, preferred_element_type=jnp.float32).astype(jnp.bfloat16)
        mixing = jnp.dot(low_rank, cross_up, preferred_element_type=jnp.float32) + cross_bias.astype(jnp.float32)
        cot_float = cot_rows.astype(jnp.float32)
        mix_grad = cot_float * cross_input.astype(jnp.float32)
        bias_part = jnp.sum(mix_grad, axis=0).astype(jnp.float32)
        rank_grad = lax.dot_general(mix_grad.astype(jnp.bfloat16), cross_up, back_dims, preferred_element_type=jnp.float32).astype(jnp.bfloat16)
        input_grad = (cot_float * (mixing + jnp.float32(1.0)) + lax.dot_general(rank_grad, cross_down, back_dims, preferred_element_type=jnp.float32)).astype(jnp.bfloat16)
        input_grad = input_grad.reshape(group, TABLES + 1, EMB)
        bottom_grad = input_grad[:, 0, :]
        shard_grads = jnp.transpose(input_grad[:, 1:, :][:, shard_table, :], (1, 0, 2))
        table_part = lax.map(grad_one, (index_block, count_block, shard_grads)).astype(jnp.float32)
        dense_parts = bottom_back(dense_rows, saved, second_layer, third_layer, bottom_grad)
        table_total, dense_total, bias_total = running
        dense_total = tuple((old + new).astype(jnp.float32) for old, new in zip(dense_total, dense_parts))
        return ((table_total + table_part).astype(jnp.float32), dense_total, (bias_total + bias_part).astype(jnp.float32)), None

    zero_dense = (zeros_float((DENSE, H1)), zeros_float((H1,)), zeros_float((H1, H2)), zeros_float((H2,)), zeros_float((H2, EMB)), zeros_float((EMB,)))
    start_state = (zeros_float((SHARDS, ROWS, EMB)), zero_dense, zeros_float((CROSS_IN,)))
    final_state, unused = lax.scan(block_step, start_state, jnp.arange(N_DP, dtype=jnp.int32))
    table_total, dense_total, bias_total = final_state
    return (table_total, dense_total[0], dense_total[1], dense_total[2], dense_total[3], dense_total[4], dense_total[5], bias_total)
```

```python
import functools

import jax
import jax.numpy as jnp
import numpy as np
from jax import lax
from jax.experimental import pallas as pl
from jax.experimental.pallas import tpu as pltpu
from jax.sharding import Mesh
from jax.sharding import PartitionSpec as P

TABLES = 26
WIDTH = 128
GROUP = 32
BLOCK = 256
LOW = 256
TABLE = ("y", "c")
DP = ("x", "z")
EVERY = ("x", "z", "y", "c")
CHUNK = 96

NT = (((1,), (1,)), ((), ()))
TN = (((0,), (0,)), ((), ()))


def dot(a, b, dims=(((1,), (0,)), ((), ()))):
    return lax.dot_general(a, b, dims, preferred_element_type=jnp.float32)


def params(megabytes=48):
    return pltpu.CompilerParams(vmem_limit_bytes=megabytes * 1024 * 1024)


def pool_kernel(code_ref, table_ref, hits_ref, pooled_ref):
    slots = code_ref.shape[2]
    rows = table_ref.shape[1]
    lane = lax.broadcasted_iota(jnp.int32, (GROUP, slots), 1)
    own = (lane & (GROUP - 1)) == lax.broadcasted_iota(jnp.int32, (GROUP, slots), 0)
    low_iota = lax.broadcasted_iota(jnp.int32, (LOW, slots), 0).astype(jnp.float32).astype(jnp.bfloat16)
    one = jnp.ones((), jnp.bfloat16)
    zero = jnp.zeros((), jnp.bfloat16)
    for group in range(BLOCK // GROUP):
        code = code_ref[0, pl.ds(group, 1), :]
        high = jnp.broadcast_to(code >> 8, (GROUP, slots))
        high = jnp.where(own, high, -1).astype(jnp.float32).astype(jnp.bfloat16)
        low = (code & (LOW - 1)).astype(jnp.float32).astype(jnp.bfloat16)
        right = jnp.where(low_iota == jnp.broadcast_to(low, (LOW, slots)), one, zero)
        left = jnp.concatenate(
            [jnp.where(high == jnp.full((), part, jnp.bfloat16), one, zero) for part in range(rows // LOW)], axis=0
        )
        hits = dot(left, right, NT).astype(jnp.bfloat16)
        for part in range(rows // LOW):
            hits_ref[0, pl.ds(group * GROUP, GROUP), pl.ds(part * LOW, LOW)] = hits[
                part * GROUP : (part + 1) * GROUP
            ]
    pooled_ref[...] = dot(hits_ref[0], table_ref[0]).astype(jnp.bfloat16)


def pool(lookup_ids, lookup_counts, embed_tables):
    shards, hot, batch = lookup_ids.shape
    rows = embed_tables.shape[1]
    slot = lax.broadcasted_iota(jnp.int32, lookup_ids.shape, 1)
    code = jnp.where(lookup_counts[:, None, :] > slot, lookup_ids, -1)
    code = code.reshape(shards, hot, batch // GROUP, GROUP).transpose(0, 2, 1, 3)
    code = code.reshape(shards, batch // GROUP, hot * GROUP)
    return pl.pallas_call(
        pool_kernel,
        grid=(shards, batch // BLOCK),
        in_specs=[
            pl.BlockSpec((1, BLOCK // GROUP, hot * GROUP), lambda s, b: (s, b, 0)),
            pl.BlockSpec((1, rows, WIDTH), lambda s, b: (s, 0, 0)),
        ],
        out_specs=[
            pl.BlockSpec((1, BLOCK, rows), lambda s, b: (s, b, 0)),
            pl.BlockSpec((BLOCK, WIDTH), lambda s, b: (b, s)),
        ],
        out_shape=[
            jax.ShapeDtypeStruct((shards, batch, rows), jnp.bfloat16),
            jax.ShapeDtypeStruct((batch, shards * WIDTH), jnp.bfloat16),
        ],
        compiler_params=params(),
        name="pool",
    )(code, embed_tables)


def table_grad_kernel(hits_ref, grad_ref, out_ref):
    total = dot(hits_ref[0], grad_ref[...], TN).astype(jnp.bfloat16)
    out_ref[...] = total.reshape(out_ref.shape)


def table_grads(hits, grads, parts):
    shards, batch, rows = hits.shape
    each = rows // parts
    step = BLOCK // each
    return pl.pallas_call(
        table_grad_kernel,
        grid=(shards, rows // BLOCK),
        in_specs=[
            pl.BlockSpec((1, batch, BLOCK), lambda s, r: (s, 0, r)),
            pl.BlockSpec((batch, WIDTH), lambda s, r: (0, s)),
        ],
        out_specs=pl.BlockSpec((step, 1, each, WIDTH), lambda s, r: (r, s, 0, 0)),
        out_shape=jax.ShapeDtypeStruct((parts, shards, each, WIDTH), jnp.bfloat16),
        compiler_params=params(),
        name="table_grads",
    )(hits, grads)


def silu(value):
    return value / (1.0 + jnp.exp(-value))


def silu_slope(value):
    sigmoid = 1.0 / (1.0 + jnp.exp(-value))
    return sigmoid * (1.0 + value * (1.0 - sigmoid))


def bottom_pre(dense, w1, b1, w2, b2, w3, b3):
    first_pre = dot(dense[...], w1[...]) + b1[...]
    first_act = silu(first_pre).astype(jnp.bfloat16)
    second_pre = dot(first_act, w2[...]) + b2[...]
    second_act = silu(second_pre).astype(jnp.bfloat16)
    third_pre = dot(second_act, w3[...]) + b3[...]
    return first_pre, first_act, second_pre, second_act, third_pre


def bottom_kernel(dense, w1, b1, w2, b2, w3, b3, out_ref):
    out_ref[...] = silu(bottom_pre(dense, w1, b1, w2, b2, w3, b3)[4]).astype(jnp.bfloat16)


def bottom_back_kernel(dense, w1, b1, w2, b2, w3, b3, grad_ref, bias_ref, out_ref):
    first_pre, first_act, second_pre, second_act, third_pre = bottom_pre(dense, w1, b1, w2, b2, w3, b3)
    third_delta = silu_slope(third_pre) * grad_ref[...].astype(jnp.float32)
    third_delta = third_delta.astype(jnp.bfloat16)
    out_ref[1024:1280, :] = dot(second_act, third_delta, TN).astype(jnp.bfloat16)
    second_delta = (silu_slope(second_pre) * dot(third_delta, w3[...], NT)).astype(jnp.bfloat16)
    second_grad = dot(first_act, second_delta, TN).astype(jnp.bfloat16)
    out_ref[0:512, :] = second_grad[:, :128]
    out_ref[512:1024, :] = second_grad[:, 128:]
    first_delta = (silu_slope(first_pre) * dot(second_delta, w2[...], NT)).astype(jnp.bfloat16)
    first_grad = dot(dense[...], first_delta, TN)
    first_grad = jnp.concatenate([first_grad, jnp.zeros((3, first_grad.shape[1]), jnp.float32)], axis=0)
    for part in range(4):
        out_ref[1280 + 16 * part : 1296 + 16 * part, :] = first_grad[:, part * 128 : part * 128 + 128].astype(
            jnp.bfloat16
        )
    first_sum = jnp.sum(first_delta.astype(jnp.float32), axis=0, keepdims=True)
    second_sum = jnp.sum(second_delta.astype(jnp.float32), axis=0, keepdims=True)
    third_sum = jnp.sum(third_delta.astype(jnp.float32), axis=0, keepdims=True)
    rows = [first_sum[:, part * 128 : part * 128 + 128] for part in range(4)]
    rows += [second_sum[:, part * 128 : part * 128 + 128] for part in range(2)]
    rows += [third_sum, jnp.zeros((9, 128), jnp.float32)]
    out_ref[1344:1360, :] = jnp.concatenate(rows, axis=0).astype(jnp.bfloat16)
    out_ref[1360:1392, :] = bias_ref[...].astype(jnp.bfloat16)
    out_ref[1392:1536, :] = jnp.zeros((144, 128), jnp.bfloat16)


def cross_kernel(
    owner_ref, arrived_ref, bottom_ref, weights_ref, bias_ref, cot_ref,
    send_ref, bottom_grad_ref, bias_grad_ref, total, inputs, mixed, grads,
):
    blocks = total.shape[0]
    wide = blocks * WIDTH
    shards = owner_ref.shape[0]
    total[1:] = jnp.zeros_like(total[1:])
    total[0] = bottom_ref[...].astype(jnp.float32)
    for shard in range(shards):
        place = owner_ref[shard] + 1
        piece = arrived_ref[shard // 2, :, (shard % 2) * WIDTH : (shard % 2) * WIDTH + WIDTH]
        total[place] = total[place] + piece.astype(jnp.float32)
    bias_grad_ref[...] = jnp.zeros_like(bias_grad_ref)
    for block in range(blocks):
        columns = slice(block * WIDTH, block * WIDTH + WIDTH)
        piece = total[block].astype(jnp.bfloat16)
        inputs[:, columns] = piece
        mix_grad = cot_ref[:, columns].astype(jnp.float32) * piece.astype(jnp.float32)
        mixed[:, columns] = mix_grad.astype(jnp.bfloat16)
        bias_grad_ref[block : block + 1, :] = jnp.sum(mix_grad, axis=0, keepdims=True)
    low_rank = dot(inputs[...], weights_ref[:, wide:], NT).astype(jnp.bfloat16)
    rank_grad = dot(mixed[...], weights_ref[:, :wide], NT).astype(jnp.bfloat16)
    step = 3 * WIDTH
    for part in range(wide // step):
        columns = slice(part * step, part * step + step)
        mixing = dot(low_rank, weights_ref[:, columns]) + bias_ref[:, columns]
        back = dot(rank_grad, weights_ref[:, wide + part * step : wide + part * step + step])
        grad = (cot_ref[:, columns].astype(jnp.float32) * (mixing + 1.0) + back).astype(jnp.bfloat16)
        for inner in range(3):
            grads[part * 3 + inner] = grad[:, inner * WIDTH : inner * WIDTH + WIDTH]
    bottom_grad_ref[...] = grads[0]
    for shard in range(shards):
        send_ref[shard // 2, :, (shard % 2) * WIDTH : (shard % 2) * WIDTH + WIDTH] = grads[owner_ref[shard] + 1]


def cross(shard_table, arrived, bottom_out, weights, cross_bias, cotangent):
    examples, wide = cotangent.shape
    blocks = wide // WIDTH
    vmem = pl.BlockSpec(memory_space=pltpu.VMEM)
    return pl.pallas_call(
        cross_kernel,
        in_specs=[pl.BlockSpec(memory_space=pltpu.SMEM)] + [vmem] * 5,
        out_specs=[vmem] * 3,
        out_shape=[
            jax.ShapeDtypeStruct(arrived.shape, jnp.bfloat16),
            jax.ShapeDtypeStruct((examples, WIDTH), jnp.bfloat16),
            jax.ShapeDtypeStruct((32, WIDTH), jnp.float32),
        ],
        scratch_shapes=[
            pltpu.VMEM((blocks, examples, WIDTH), jnp.float32),
            pltpu.VMEM((examples, wide), jnp.bfloat16),
            pltpu.VMEM((examples, wide), jnp.bfloat16),
            pltpu.VMEM((blocks, examples, WIDTH), jnp.bfloat16),
        ],
        compiler_params=params(),
        name="cross",
    )(shard_table, arrived, bottom_out, weights, cross_bias, cotangent)


def local(
    dense_feats, lookup_ids, lookup_counts, shard_table, embed_tables, first_layer, first_offset, second_layer,
    second_offset, third_layer, third_offset, cross_down, cross_up, cross_bias, cotangent,
):
    examples = dense_feats.shape[0]
    devices = lookup_ids.shape[2] // examples
    weights = lax.all_gather(jnp.concatenate([cross_up, cross_down.T], axis=1), TABLE, axis=0, tiled=True)
    hits, pooled = pool(lookup_ids, lookup_counts, embed_tables)
    pooled = pooled.reshape(devices, examples, pooled.shape[1])
    arrived = lax.all_to_all(pooled, TABLE, split_axis=0, concat_axis=0, tiled=True)
    vmem = pl.BlockSpec(memory_space=pltpu.VMEM)
    bottom_args = (
        dense_feats, first_layer, first_offset[None], second_layer, second_offset[None], third_layer,
        third_offset[None],
    )
    bottom_out = pl.pallas_call(
        bottom_kernel,
        in_specs=[vmem] * 7,
        out_specs=vmem,
        out_shape=jax.ShapeDtypeStruct((examples, WIDTH), jnp.bfloat16),
        compiler_params=params(),
        name="bottom",
    )(*bottom_args)
    send, bottom_grad, bias_part = cross(shard_table, arrived, bottom_out, weights, cross_bias[None], cotangent)
    returned = lax.all_to_all(send, TABLE, split_axis=0, concat_axis=0, tiled=True)
    parts = lax.axis_size("x") * lax.axis_size("z")
    table_parts = table_grads(hits, returned.reshape(-1, returned.shape[2]), parts)
    table_parts = lax.all_to_all(table_parts, DP, split_axis=0, concat_axis=0, tiled=True)
    table_grad = jnp.sum(table_parts.astype(jnp.float32), axis=0)

    packed = pl.pallas_call(
        bottom_back_kernel,
        in_specs=[vmem] * 9,
        out_specs=vmem,
        out_shape=jax.ShapeDtypeStruct((devices * CHUNK, 128), jnp.bfloat16),
        compiler_params=params(),
        name="bottom_back",
    )(*bottom_args, bottom_grad, bias_part)
    packed = lax.all_to_all(packed.reshape(devices, CHUNK, 128), TABLE, split_axis=0, concat_axis=0, tiled=True)
    summed = jnp.sum(packed.astype(jnp.float32), axis=0)
    summed = lax.psum(lax.psum(summed, "x"), "z").astype(jnp.bfloat16)
    summed = lax.all_gather(summed, TABLE, axis=0, tiled=True)
    whole = summed.astype(jnp.float32)
    second_grad = jnp.concatenate([whole[0:512], whole[512:1024]], axis=1)
    first_grad = jnp.concatenate([whole[1280 + 16 * part : 1293 + 16 * part] for part in range(4)], axis=1)
    return (
        table_grad,
        first_grad,
        whole[1344:1348].reshape(-1),
        second_grad,
        whole[1348:1350].reshape(-1),
        whole[1024:1280],
        whole[1350],
        whole[1360:1387].reshape(-1),
    )


def solution(mesh):
    fine = Mesh(mesh.devices.reshape(4, 8, 8, 2), EVERY)
    placed = (
        P(EVERY, None),
        P(TABLE, None, DP),
        P(TABLE, DP),
        P(),
        P(TABLE, None, None),
        P(),
        P(),
        P(),
        P(),
        P(),
        P(),
        P(None, TABLE),
        P(TABLE, None),
        P(),
        P(EVERY, None),
    )
    return jax.shard_map(
        local,
        mesh=fine,
        in_specs=placed,
        out_specs=(P(TABLE, DP, None), P(), P(), P(), P(), P(), P(), P()),
        check_vma=False,
    )
```

```python
import functools

import jax
import jax.numpy as jnp
import numpy as np
from jax import lax
from jax.experimental import pallas as pl
from jax.experimental.pallas import tpu as pltpu
from jax.sharding import Mesh
from jax.sharding import PartitionSpec as P

TABLES = 26
WIDTH = 128
GROUP = 32
BLOCK = 256
LOW = 256
TABLE = ("y", "c")
DP = ("x", "z")
EVERY = ("x", "z", "y", "c")
CHUNK = 192

NT = (((1,), (1,)), ((), ()))
TN = (((0,), (0,)), ((), ()))


def dot(a, b, dims=(((1,), (0,)), ((), ()))):
    return lax.dot_general(a, b, dims, preferred_element_type=jnp.float32)


def params(megabytes):
    return pltpu.CompilerParams(vmem_limit_bytes=megabytes * 1024 * 1024)


def pool_kernel(code_ref, table_ref, hits_ref, pooled_ref):
    slots = code_ref.shape[2]
    rows = table_ref.shape[1]
    lane = lax.broadcasted_iota(jnp.int32, (GROUP, slots), 1)
    own = (lane & (GROUP - 1)) == lax.broadcasted_iota(jnp.int32, (GROUP, slots), 0)
    low_iota = lax.broadcasted_iota(jnp.int32, (LOW, slots), 0).astype(jnp.float32).astype(jnp.bfloat16)
    one = jnp.ones((), jnp.bfloat16)
    zero = jnp.zeros((), jnp.bfloat16)
    for group in range(BLOCK // GROUP):
        code = code_ref[0, pl.ds(group, 1), :]
        high = jnp.broadcast_to(code >> 8, (GROUP, slots))
        high = jnp.where(own, high, -1).astype(jnp.float32).astype(jnp.bfloat16)
        low = (code & (LOW - 1)).astype(jnp.float32).astype(jnp.bfloat16)
        right = jnp.where(low_iota == jnp.broadcast_to(low, (LOW, slots)), one, zero)
        left = jnp.concatenate(
            [jnp.where(high == jnp.full((), part, jnp.bfloat16), one, zero) for part in range(rows // LOW)], axis=0
        )
        hits = dot(left, right, NT).astype(jnp.bfloat16)
        for part in range(rows // LOW):
            hits_ref[0, part, pl.ds(group * GROUP, GROUP), :] = hits[part * GROUP : (part + 1) * GROUP]
    total = dot(hits_ref[0, 0], table_ref[0, 0:LOW])
    for part in range(1, rows // LOW):
        total = total + dot(hits_ref[0, part], table_ref[0, part * LOW : part * LOW + LOW])
    pooled_ref[...] = total.astype(jnp.bfloat16)


def pool(lookup_ids, lookup_counts, embed_tables):
    shards, hot, batch = lookup_ids.shape
    rows = embed_tables.shape[1]
    slot = lax.broadcasted_iota(jnp.int32, lookup_ids.shape, 1)
    code = jnp.where(lookup_counts[:, None, :] > slot, lookup_ids, -1)
    code = code.reshape(shards, hot, batch // GROUP, GROUP).transpose(0, 2, 1, 3)
    code = code.reshape(shards, batch // GROUP, hot * GROUP)
    return pl.pallas_call(
        pool_kernel,
        grid=(shards, batch // BLOCK),
        in_specs=[
            pl.BlockSpec((1, BLOCK // GROUP, hot * GROUP), lambda s, b: (s, b, 0)),
            pl.BlockSpec((1, rows, WIDTH), lambda s, b: (s, 0, 0)),
        ],
        out_specs=[
            pl.BlockSpec((1, rows // LOW, BLOCK, LOW), lambda s, b: (s, 0, b, 0)),
            pl.BlockSpec((BLOCK, WIDTH), lambda s, b: (b, s)),
        ],
        out_shape=[
            pltpu.HBM((shards, rows // LOW, batch, LOW), jnp.bfloat16),
            jax.ShapeDtypeStruct((batch, shards * WIDTH), jnp.bfloat16),
        ],
        compiler_params=params(8),
        name="pool",
    )(code, embed_tables)


def table_grad_kernel(hits_ref, grad_ref, out_ref, turned):
    @pl.when(pl.program_id(0) == 0)
    def _():
        turned[...] = grad_ref[...].T

    total = dot(turned[...], hits_ref[0, 0]).T.astype(jnp.bfloat16)
    out_ref[...] = total.reshape(out_ref.shape)


def table_grads(hits, grads, shard, parts, extra=()):
    shards, blocks, batch, low = hits.shape
    each = blocks * low // parts
    step = low // each
    hbm = pl.BlockSpec(memory_space=pl.ANY)

    def kernel(hits_ref, grad_ref, *rest):
        table_grad_kernel(hits_ref, grad_ref, rest[-2], rest[-1])

    return pl.pallas_call(
        kernel,
        grid=(blocks,),
        in_specs=[
            pl.BlockSpec((1, 1, batch, low), lambda r: (shard, r, 0, 0)),
            pl.BlockSpec((batch, WIDTH), lambda r: (0, shard)),
        ]
        + [hbm] * len(extra),
        out_specs=pl.BlockSpec((step, 1, each, WIDTH), lambda r: (r, shard, 0, 0)),
        out_shape=jax.ShapeDtypeStruct((parts, shards, each, WIDTH), jnp.bfloat16),
        scratch_shapes=[pltpu.VMEM((WIDTH, batch), jnp.bfloat16)],
        input_output_aliases={2: 0} if shard else {},
        compiler_params=params(46),
        cost_estimate=pl.CostEstimate(
            flops=2 * batch * blocks * low * WIDTH, bytes_accessed=2 * batch * (blocks * low + 2 * WIDTH), transcendentals=0
        ),
        name="table_grads",
    )(hits, grads, *extra)


def silu(value):
    return value / (1.0 + jnp.exp(-value))


def silu_slope(value):
    sigmoid = 1.0 / (1.0 + jnp.exp(-value))
    return sigmoid * (1.0 + value * (1.0 - sigmoid))


def bottom_pre(dense, w1, b1, w2, b2, w3, b3):
    first_pre = dot(dense[...], w1[...]) + b1[...]
    first_act = silu(first_pre).astype(jnp.bfloat16)
    second_pre = dot(first_act, w2[...]) + b2[...]
    second_act = silu(second_pre).astype(jnp.bfloat16)
    third_pre = dot(second_act, w3[...]) + b3[...]
    return first_pre, first_act, second_pre, second_act, third_pre


def bottom_kernel(dense, w1, b1, w2, b2, w3, b3, out_ref):
    out_ref[...] = silu(bottom_pre(dense, w1, b1, w2, b2, w3, b3)[4]).astype(jnp.bfloat16)


def bottom_back_kernel(dense, w1, b1, w2, b2, w3, b3, grad_ref, bias_ref, out_ref):
    first_pre, first_act, second_pre, second_act, third_pre = bottom_pre(dense, w1, b1, w2, b2, w3, b3)
    third_delta = silu_slope(third_pre) * grad_ref[...].astype(jnp.float32)
    third_delta = third_delta.astype(jnp.bfloat16)
    out_ref[1024:1280, :] = dot(second_act, third_delta, TN).astype(jnp.bfloat16)
    second_delta = (silu_slope(second_pre) * dot(third_delta, w3[...], NT)).astype(jnp.bfloat16)
    second_grad = dot(first_act, second_delta, TN).astype(jnp.bfloat16)
    out_ref[0:512, :] = second_grad[:, :128]
    out_ref[512:1024, :] = second_grad[:, 128:]
    first_delta = (silu_slope(first_pre) * dot(second_delta, w2[...], NT)).astype(jnp.bfloat16)
    first_grad = dot(dense[...], first_delta, TN)
    first_grad = jnp.concatenate([first_grad, jnp.zeros((3, first_grad.shape[1]), jnp.float32)], axis=0)
    for part in range(4):
        out_ref[1280 + 16 * part : 1296 + 16 * part, :] = first_grad[:, part * 128 : part * 128 + 128].astype(
            jnp.bfloat16
        )
    first_sum = jnp.sum(first_delta.astype(jnp.float32), axis=0, keepdims=True)
    second_sum = jnp.sum(second_delta.astype(jnp.float32), axis=0, keepdims=True)
    third_sum = jnp.sum(third_delta.astype(jnp.float32), axis=0, keepdims=True)
    rows = [first_sum[:, part * 128 : part * 128 + 128] for part in range(4)]
    rows += [second_sum[:, part * 128 : part * 128 + 128] for part in range(2)]
    rows += [third_sum, jnp.zeros((9, 128), jnp.float32)]
    out_ref[1344:1360, :] = jnp.concatenate(rows, axis=0).astype(jnp.bfloat16)
    out_ref[1360:1392, :] = bias_ref[...].astype(jnp.bfloat16)
    out_ref[1392:1536, :] = jnp.zeros((144, 128), jnp.bfloat16)


def unpack_kernel(whole, first_grad, second_grad, third_grad, first_sum, second_sum, third_sum, bias_sum):
    second_grad[:, 0:128] = whole[0:512].astype(jnp.float32)
    second_grad[:, 128:256] = whole[512:1024].astype(jnp.float32)
    third_grad[...] = whole[1024:1280].astype(jnp.float32)
    for part in range(4):
        block = whole[1280 + 16 * part : 1296 + 16 * part].astype(jnp.float32)
        first_grad[:, part * 128 : part * 128 + 128] = block[0:13]
    sums = whole[1344:1360].astype(jnp.float32)
    for part in range(4):
        first_sum[:, part * 128 : part * 128 + 128] = sums[part : part + 1]
    for part in range(2):
        second_sum[:, part * 128 : part * 128 + 128] = sums[4 + part : 5 + part]
    third_sum[...] = sums[6:7]
    biases = whole[1360:1392].astype(jnp.float32)
    for part in range(27):
        bias_sum[:, part * 128 : part * 128 + 128] = biases[part : part + 1]


def cross_kernel(
    owner_ref, arrived_ref, bottom_ref, weights_ref, bias_ref, cot_ref,
    send_ref, bottom_grad_ref, bias_grad_ref, total, inputs, mixed, grads, up, down, arrived_at,
):
    blocks = total.shape[0]
    wide = blocks * WIDTH
    shards = owner_ref.shape[0]
    fetch_down = pltpu.make_async_copy(weights_ref.at[:, wide : 2 * wide], down, arrived_at.at[0])
    fetch_up = pltpu.make_async_copy(weights_ref.at[:, 0:wide], up, arrived_at.at[1])
    fetch_down.start()
    fetch_up.start()
    total[1:] = jnp.zeros_like(total[1:])
    total[0] = bottom_ref[...].astype(jnp.float32)
    for shard in range(shards):
        place = owner_ref[shard] + 1
        piece = arrived_ref[shard // 2, :, (shard % 2) * WIDTH : (shard % 2) * WIDTH + WIDTH]
        total[place] = total[place] + piece.astype(jnp.float32)
    bias_grad_ref[...] = jnp.zeros_like(bias_grad_ref)
    for block in range(blocks):
        columns = slice(block * WIDTH, block * WIDTH + WIDTH)
        piece = total[block].astype(jnp.bfloat16)
        inputs[:, columns] = piece
        mix_grad = cot_ref[:, columns].astype(jnp.float32) * piece.astype(jnp.float32)
        mixed[:, columns] = mix_grad.astype(jnp.bfloat16)
        bias_grad_ref[block : block + 1, :] = jnp.sum(mix_grad, axis=0, keepdims=True)
    fetch_down.wait()
    low_rank = dot(inputs[...], down[...], NT).astype(jnp.bfloat16)
    fetch_up.wait()
    rank_grad = dot(mixed[...], up[...], NT).astype(jnp.bfloat16)
    step = 3 * WIDTH
    for part in range(wide // step):
        columns = slice(part * step, part * step + step)
        mixing = dot(low_rank, up[:, columns]) + bias_ref[:, columns]
        back = dot(rank_grad, down[:, columns])
        grad = (cot_ref[:, columns].astype(jnp.float32) * (mixing + 1.0) + back).astype(jnp.bfloat16)
        for inner in range(3):
            grads[part * 3 + inner] = grad[:, inner * WIDTH : inner * WIDTH + WIDTH]
    bottom_grad_ref[...] = grads[0]
    for shard in range(shards):
        send_ref[shard // 2, :, (shard % 2) * WIDTH : (shard % 2) * WIDTH + WIDTH] = grads[owner_ref[shard] + 1]


def cross(shard_table, arrived, bottom_out, weights, cross_bias, cotangent):
    examples, wide = cotangent.shape
    blocks = wide // WIDTH
    vmem = pl.BlockSpec(memory_space=pltpu.VMEM)
    return pl.pallas_call(
        cross_kernel,
        in_specs=[pl.BlockSpec(memory_space=pltpu.SMEM), vmem, vmem, pl.BlockSpec(memory_space=pltpu.HBM), vmem, vmem],
        out_specs=[vmem] * 3,
        out_shape=[
            jax.ShapeDtypeStruct(arrived.shape, jnp.bfloat16),
            jax.ShapeDtypeStruct((examples, WIDTH), jnp.bfloat16),
            jax.ShapeDtypeStruct((32, WIDTH), jnp.float32),
        ],
        scratch_shapes=[
            pltpu.VMEM((blocks, examples, WIDTH), jnp.float32),
            pltpu.VMEM((examples, wide), jnp.bfloat16),
            pltpu.VMEM((examples, wide), jnp.bfloat16),
            pltpu.VMEM((blocks, examples, WIDTH), jnp.bfloat16),
            pltpu.VMEM((weights.shape[0], wide), jnp.bfloat16),
            pltpu.VMEM((weights.shape[0], wide), jnp.bfloat16),
            pltpu.SemaphoreType.DMA((2,)),
        ],
        compiler_params=params(55),
        name="cross",
    )(shard_table, arrived, bottom_out, weights, cross_bias, cotangent)


def spread_sum(value, axis, distances, after=None):
    size = lax.axis_size(axis)
    for distance in distances:
        sent = value.astype(jnp.bfloat16)
        came = lax.ppermute(sent, axis, [(place, place ^ distance) for place in range(size)])
        if after is None:
            value = sent.astype(jnp.float32) + came.astype(jnp.float32)
        else:
            value = add_after(sent, came, after)
    return value


def add_kernel(one_ref, other_ref, after_ref, out_ref):
    out_ref[...] = (one_ref[...].astype(jnp.float32) + other_ref[...].astype(jnp.float32)).astype(jnp.bfloat16)


def add_after(one, other, after):
    vmem = pl.BlockSpec(memory_space=pltpu.VMEM)
    return pl.pallas_call(
        add_kernel,
        in_specs=[vmem, vmem, pl.BlockSpec(memory_space=pl.ANY)],
        out_specs=vmem,
        out_shape=jax.ShapeDtypeStruct(one.shape, jnp.bfloat16),
        compiler_params=params(4),
        name="add_after",
    )(one, other, after)


def hold(value, after):
    anywhere = pl.BlockSpec(memory_space=pl.ANY)

    def kernel(value_ref, after_ref, out_ref):
        pass

    return pl.pallas_call(
        kernel,
        in_specs=[anywhere, anywhere],
        out_specs=anywhere,
        out_shape=jax.ShapeDtypeStruct(value.shape, value.dtype),
        input_output_aliases={0: 0},
        compiler_params=params(4),
        name="hold",
    )(value, after)


def local(
    dense_feats, lookup_ids, lookup_counts, shard_table, embed_tables, first_layer, first_offset, second_layer,
    second_offset, third_layer, third_offset, cross_down, cross_up, cross_bias, cotangent,
):
    examples = dense_feats.shape[0]
    devices = lookup_ids.shape[2] // examples
    weights = lax.all_gather(jnp.concatenate([cross_up, cross_down.T], axis=1), TABLE, axis=0, tiled=True)
    hits, pooled = pool(lookup_ids, lookup_counts, embed_tables)
    pooled = pooled.reshape(devices, examples, pooled.shape[1])
    arrived = lax.all_to_all(pooled, TABLE, split_axis=0, concat_axis=0, tiled=True)
    vmem = pl.BlockSpec(memory_space=pltpu.VMEM)
    bottom_args = (
        dense_feats, first_layer, first_offset[None], second_layer, second_offset[None], third_layer,
        third_offset[None],
    )
    bottom_out = pl.pallas_call(
        bottom_kernel,
        in_specs=[vmem] * 7,
        out_specs=vmem,
        out_shape=jax.ShapeDtypeStruct((examples, WIDTH), jnp.bfloat16),
        compiler_params=params(8),
        name="bottom",
    )(*bottom_args)
    send, bottom_grad, bias_part = cross(shard_table, arrived, bottom_out, weights, cross_bias[None], cotangent)
    returned = lax.all_to_all(send, TABLE, split_axis=0, concat_axis=0, tiled=True)
    parts = lax.axis_size("x") * lax.axis_size("z")
    packed = pl.pallas_call(
        bottom_back_kernel,
        in_specs=[vmem] * 9,
        out_specs=vmem,
        out_shape=jax.ShapeDtypeStruct((8 * CHUNK, 128), jnp.bfloat16),
        compiler_params=params(8),
        name="bottom_back",
    )(*bottom_args, bottom_grad, bias_part)
    core, column = lax.axis_index("c"), lax.axis_index("x")
    length = lax.axis_size("x")
    packed = packed.reshape(length, 2, CHUNK, 128)
    theirs = lax.dynamic_index_in_dim(packed, 1 - core, axis=1, keepdims=False)
    came = lax.ppermute(theirs, "c", [(0, 1), (1, 0)])
    mine = lax.dynamic_index_in_dim(packed, core, axis=1, keepdims=False)
    both = mine.astype(jnp.float32) + came.astype(jnp.float32)
    part = lax.dynamic_index_in_dim(both, column, axis=0, keepdims=False)
    narrow = both.astype(jnp.bfloat16)
    for shift in range(1, length):
        piece = lax.dynamic_index_in_dim(narrow, (column + shift) % length, axis=0, keepdims=False)
        piece = lax.ppermute(piece, "x", [(place, (place + shift) % length) for place in range(length)])
        part = part + piece.astype(jnp.float32)
    part = spread_sum(part, "z", (1,))
    part = spread_sum(part, "z", (2,), returned)
    part = spread_sum(part, "z", (4,))

    returned = returned.reshape(-1, returned.shape[2])
    table_parts = table_grads(hits, returned, 0, parts)
    for shard in range(1, hits.shape[0]):
        table_parts = table_grads(hits, returned, shard, parts, (table_parts, part))
    part = spread_sum(part, "y", (1,))
    table_parts = hold(table_parts, part)
    table_parts = lax.all_to_all(table_parts, DP, split_axis=0, concat_axis=0, tiled=True)
    table_grad = jnp.sum(table_parts.astype(jnp.float32), axis=0)

    part = spread_sum(part, "y", (2, 4)).astype(jnp.bfloat16)
    other = lax.ppermute(part, "c", [(0, 1), (1, 0)])
    pair = jnp.where(core == 0, jnp.stack([part, other]), jnp.stack([other, part]))
    whole = lax.all_gather(pair.reshape(2 * CHUNK, 128), "x", axis=0, tiled=True)
    first_grad, second_grad, third_grad, first_sum, second_sum, third_sum, bias_sum = pl.pallas_call(
        unpack_kernel,
        in_specs=[vmem],
        out_specs=[vmem] * 7,
        out_shape=[
            jax.ShapeDtypeStruct(shape, jnp.float32)
            for shape in (
                first_layer.shape, second_layer.shape, third_layer.shape, (1, first_layer.shape[1]),
                (1, second_layer.shape[1]), (1, third_layer.shape[1]), (1, cross_bias.shape[0]),
            )
        ],
        compiler_params=params(8),
        name="unpack",
    )(whole)
    return (
        table_grad, first_grad, first_sum[0], second_grad, second_sum[0], third_grad, third_sum[0], bias_sum[0],
    )


def solution(mesh):
    fine = Mesh(mesh.devices.reshape(4, 8, 8, 2), EVERY)
    placed = (
        P(EVERY, None),
        P(TABLE, None, DP),
        P(TABLE, DP),
        P(),
        P(TABLE, None, None),
        P(),
        P(),
        P(),
        P(),
        P(),
        P(),
        P(None, TABLE),
        P(TABLE, None),
        P(),
        P(EVERY, None),
    )
    return jax.shard_map(
        local,
        mesh=fine,
        in_specs=placed,
        out_specs=(P(TABLE, DP, None), P(), P(), P(), P(), P(), P(), P()),
        check_vma=False,
    )
```

```python
import math

import jax
import jax.numpy as jnp
from jax import lax
from jax.experimental import pallas as pl
from jax.experimental.pallas import tpu as pltpu
from jax.sharding import Mesh
from jax.sharding import PartitionSpec as P

TABLES = 26
WIDTH = 128
GROUP = 32
BLOCK = 256
LOW = 256
TABLE = ("yh", "yl", "c")
DP = ("x", "zh", "zl")
EVERY = ("x", "zh", "zl", "yh", "yl", "c")
CHUNK = 192

NT = (((1,), (1,)), ((), ()))
TN = (((0,), (0,)), ((), ()))


def dot(a, b, dims=(((1,), (0,)), ((), ()))):
    return lax.dot_general(a, b, dims, preferred_element_type=jnp.float32)


def params(megabytes):
    return pltpu.CompilerParams(vmem_limit_bytes=megabytes * 1024 * 1024)


def pool_kernel(code_ref, table_ref, hits_ref, pooled_ref):
    slots = code_ref.shape[2]
    rows = table_ref.shape[1]
    lane = lax.broadcasted_iota(jnp.int32, (GROUP, slots), 1)
    own = (lane & (GROUP - 1)) == lax.broadcasted_iota(jnp.int32, (GROUP, slots), 0)
    low_iota = lax.broadcasted_iota(jnp.int32, (LOW, slots), 0).astype(jnp.float32).astype(jnp.bfloat16)
    one = jnp.ones((), jnp.bfloat16)
    zero = jnp.zeros((), jnp.bfloat16)
    for group in range(BLOCK // GROUP):
        code = code_ref[0, pl.ds(group, 1), :]
        high = jnp.broadcast_to(code >> 8, (GROUP, slots))
        high = jnp.where(own, high, -1).astype(jnp.float32).astype(jnp.bfloat16)
        low = (code & (LOW - 1)).astype(jnp.float32).astype(jnp.bfloat16)
        right = jnp.where(low_iota == jnp.broadcast_to(low, (LOW, slots)), one, zero)
        left = jnp.concatenate(
            [jnp.where(high == jnp.full((), part, jnp.bfloat16), one, zero) for part in range(rows // LOW)], axis=0
        )
        hits = dot(left, right, NT).astype(jnp.bfloat16)
        for part in range(rows // LOW):
            hits_ref[0, part, pl.ds(group * GROUP, GROUP), :] = hits[part * GROUP : (part + 1) * GROUP]
    total = dot(hits_ref[0, 0], table_ref[0, 0:LOW])
    for part in range(1, rows // LOW):
        total = total + dot(hits_ref[0, part], table_ref[0, part * LOW : part * LOW + LOW])
    pooled_ref[...] = total.astype(jnp.bfloat16)


def pool(lookup_ids, lookup_counts, embed_tables):
    shards, hot, batch = lookup_ids.shape
    rows = embed_tables.shape[1]
    slot = lax.broadcasted_iota(jnp.int32, lookup_ids.shape, 1)
    code = jnp.where(lookup_counts[:, None, :] > slot, lookup_ids, -1)
    code = code.reshape(shards, hot, batch // GROUP, GROUP).transpose(0, 2, 1, 3)
    code = code.reshape(shards, batch // GROUP, hot * GROUP)
    return pl.pallas_call(
        pool_kernel,
        grid=(shards, batch // BLOCK),
        in_specs=[
            pl.BlockSpec((1, BLOCK // GROUP, hot * GROUP), lambda s, b: (s, b, 0)),
            pl.BlockSpec((1, rows, WIDTH), lambda s, b: (s, 0, 0)),
        ],
        out_specs=[
            pl.BlockSpec((1, rows // LOW, BLOCK, LOW), lambda s, b: (s, 0, b, 0)),
            pl.BlockSpec((BLOCK, WIDTH), lambda s, b: (b, s)),
        ],
        out_shape=[
            pltpu.HBM((shards, rows // LOW, batch, LOW), jnp.bfloat16),
            jax.ShapeDtypeStruct((batch, shards * WIDTH), jnp.bfloat16),
        ],
        compiler_params=params(8),
        name="pool",
    )(code, embed_tables)


def table_grad_kernel(hits_ref, grad_ref, out_ref, turned):
    @pl.when(pl.program_id(1) == 0)
    def _():
        turned[...] = grad_ref[...].T

    blocks = hits_ref.shape[1]
    step = out_ref.shape[0] // blocks
    for block in range(blocks):
        total = dot(turned[...], hits_ref[0, block]).T.astype(jnp.bfloat16)
        out_ref[block * step : block * step + step] = total.reshape(step, *out_ref.shape[1:])


def table_grads(hits, grads, parts):
    shards, blocks, batch, low = hits.shape
    each = blocks * low // parts
    wide = math.gcd(blocks, 4)
    step = wide * low // each
    return pl.pallas_call(
        table_grad_kernel,
        grid=(shards, blocks // wide),
        in_specs=[
            pl.BlockSpec((1, wide, batch, low), lambda s, r: (s, r, 0, 0)),
            pl.BlockSpec((batch, WIDTH), lambda s, r: (0, s)),
        ],
        out_specs=pl.BlockSpec((step, 1, each, WIDTH), lambda s, r: (r, s, 0, 0)),
        out_shape=jax.ShapeDtypeStruct((parts, shards, each, WIDTH), jnp.bfloat16),
        scratch_shapes=[pltpu.VMEM((WIDTH, batch), jnp.bfloat16)],
        compiler_params=params(46),
        cost_estimate=pl.CostEstimate(
            flops=2 * shards * batch * blocks * low * WIDTH,
            bytes_accessed=2 * shards * batch * (blocks * low + 2 * WIDTH),
            transcendentals=0,
        ),
        name="table_grads",
    )(hits, grads)


def silu(value):
    return value / (1.0 + jnp.exp(-value))


def silu_slope(value):
    sigmoid = 1.0 / (1.0 + jnp.exp(-value))
    return sigmoid * (1.0 + value * (1.0 - sigmoid))


def bottom_pre(dense, w1, b1, w2, b2, w3, b3):
    first_pre = dot(dense[...], w1[...]) + b1[...]
    first_act = silu(first_pre).astype(jnp.bfloat16)
    second_pre = dot(first_act, w2[...]) + b2[...]
    second_act = silu(second_pre).astype(jnp.bfloat16)
    third_pre = dot(second_act, w3[...]) + b3[...]
    return first_pre, first_act, second_pre, second_act, third_pre


def bottom_kernel(dense, w1, b1, w2, b2, w3, b3, out_ref):
    out_ref[...] = silu(bottom_pre(dense, w1, b1, w2, b2, w3, b3)[4]).astype(jnp.bfloat16)


def bottom_back_kernel(dense, w1, b1, w2, b2, w3, b3, grad_ref, bias_ref, out_ref):
    first_pre, first_act, second_pre, second_act, third_pre = bottom_pre(dense, w1, b1, w2, b2, w3, b3)
    third_delta = silu_slope(third_pre) * grad_ref[...].astype(jnp.float32)
    third_delta = third_delta.astype(jnp.bfloat16)
    out_ref[1024:1280, :] = dot(second_act, third_delta, TN).astype(jnp.bfloat16)
    second_delta = (silu_slope(second_pre) * dot(third_delta, w3[...], NT)).astype(jnp.bfloat16)
    second_grad = dot(first_act, second_delta, TN).astype(jnp.bfloat16)
    out_ref[0:512, :] = second_grad[:, :128]
    out_ref[512:1024, :] = second_grad[:, 128:]
    first_delta = (silu_slope(first_pre) * dot(second_delta, w2[...], NT)).astype(jnp.bfloat16)
    first_grad = dot(dense[...], first_delta, TN)
    first_grad = jnp.concatenate([first_grad, jnp.zeros((3, first_grad.shape[1]), jnp.float32)], axis=0)
    for part in range(4):
        out_ref[1280 + 16 * part : 1296 + 16 * part, :] = first_grad[:, part * 128 : part * 128 + 128].astype(
            jnp.bfloat16
        )
    first_sum = jnp.sum(first_delta.astype(jnp.float32), axis=0, keepdims=True)
    second_sum = jnp.sum(second_delta.astype(jnp.float32), axis=0, keepdims=True)
    third_sum = jnp.sum(third_delta.astype(jnp.float32), axis=0, keepdims=True)
    rows = [first_sum[:, part * 128 : part * 128 + 128] for part in range(4)]
    rows += [second_sum[:, part * 128 : part * 128 + 128] for part in range(2)]
    rows += [third_sum, jnp.zeros((9, 128), jnp.float32)]
    out_ref[1344:1360, :] = jnp.concatenate(rows, axis=0).astype(jnp.bfloat16)
    out_ref[1360:1392, :] = bias_ref[...].astype(jnp.bfloat16)
    out_ref[1392:1536, :] = jnp.zeros((144, 128), jnp.bfloat16)


def unpack_kernel(whole, first_grad, second_grad, third_grad, first_sum, second_sum, third_sum, bias_sum):
    second_grad[:, 0:128] = whole[0:512].astype(jnp.float32)
    second_grad[:, 128:256] = whole[512:1024].astype(jnp.float32)
    third_grad[...] = whole[1024:1280].astype(jnp.float32)
    for part in range(4):
        block = whole[1280 + 16 * part : 1296 + 16 * part].astype(jnp.float32)
        first_grad[:, part * 128 : part * 128 + 128] = block[0:13]
    sums = whole[1344:1360].astype(jnp.float32)
    for part in range(4):
        first_sum[:, part * 128 : part * 128 + 128] = sums[part : part + 1]
    for part in range(2):
        second_sum[:, part * 128 : part * 128 + 128] = sums[4 + part : 5 + part]
    third_sum[...] = sums[6:7]
    biases = whole[1360:1392].astype(jnp.float32)
    for part in range(27):
        bias_sum[:, part * 128 : part * 128 + 128] = biases[part : part + 1]


def cross_kernel(
    owner_ref, arrived_ref, bottom_ref, weights_ref, bias_ref, cot_ref,
    send_ref, bottom_grad_ref, bias_grad_ref, total, inputs, mixed, grads, up, down, arrived_at,
):
    blocks = total.shape[0]
    wide = blocks * WIDTH
    shards = owner_ref.shape[0]
    fetch_down = pltpu.make_async_copy(weights_ref.at[:, wide : 2 * wide], down, arrived_at.at[0])
    fetch_up = pltpu.make_async_copy(weights_ref.at[:, 0:wide], up, arrived_at.at[1])
    fetch_down.start()
    fetch_up.start()
    total[1:] = jnp.zeros_like(total[1:])
    total[0] = bottom_ref[...].astype(jnp.float32)
    for shard in range(shards):
        place = owner_ref[shard] + 1
        piece = arrived_ref[shard // 2, :, (shard % 2) * WIDTH : (shard % 2) * WIDTH + WIDTH]
        total[place] = total[place] + piece.astype(jnp.float32)
    bias_grad_ref[...] = jnp.zeros_like(bias_grad_ref)
    for block in range(blocks):
        columns = slice(block * WIDTH, block * WIDTH + WIDTH)
        piece = total[block].astype(jnp.bfloat16)
        inputs[:, columns] = piece
        mix_grad = cot_ref[:, columns].astype(jnp.float32) * piece.astype(jnp.float32)
        mixed[:, columns] = mix_grad.astype(jnp.bfloat16)
        bias_grad_ref[block : block + 1, :] = jnp.sum(mix_grad, axis=0, keepdims=True)
    fetch_down.wait()
    low_rank = dot(inputs[...], down[...], NT).astype(jnp.bfloat16)
    fetch_up.wait()
    rank_grad = dot(mixed[...], up[...], NT).astype(jnp.bfloat16)
    step = 3 * WIDTH
    for part in range(wide // step):
        columns = slice(part * step, part * step + step)
        mixing = dot(low_rank, up[:, columns]) + bias_ref[:, columns]
        back = dot(rank_grad, down[:, columns])
        grad = (cot_ref[:, columns].astype(jnp.float32) * (mixing + 1.0) + back).astype(jnp.bfloat16)
        for inner in range(3):
            grads[part * 3 + inner] = grad[:, inner * WIDTH : inner * WIDTH + WIDTH]
    bottom_grad_ref[...] = grads[0]
    for shard in range(shards):
        send_ref[shard // 2, :, (shard % 2) * WIDTH : (shard % 2) * WIDTH + WIDTH] = grads[owner_ref[shard] + 1]


def cross(shard_table, arrived, bottom_out, weights, cross_bias, cotangent):
    examples, wide = cotangent.shape
    blocks = wide // WIDTH
    vmem = pl.BlockSpec(memory_space=pltpu.VMEM)
    return pl.pallas_call(
        cross_kernel,
        in_specs=[pl.BlockSpec(memory_space=pltpu.SMEM), vmem, vmem, pl.BlockSpec(memory_space=pltpu.HBM), vmem, vmem],
        out_specs=[vmem] * 3,
        out_shape=[
            jax.ShapeDtypeStruct(arrived.shape, jnp.bfloat16),
            jax.ShapeDtypeStruct((examples, WIDTH), jnp.bfloat16),
            jax.ShapeDtypeStruct((32, WIDTH), jnp.float32),
        ],
        scratch_shapes=[
            pltpu.VMEM((blocks, examples, WIDTH), jnp.float32),
            pltpu.VMEM((examples, wide), jnp.bfloat16),
            pltpu.VMEM((examples, wide), jnp.bfloat16),
            pltpu.VMEM((blocks, examples, WIDTH), jnp.bfloat16),
            pltpu.VMEM((weights.shape[0], wide), jnp.bfloat16),
            pltpu.VMEM((weights.shape[0], wide), jnp.bfloat16),
            pltpu.SemaphoreType.DMA((2,)),
        ],
        compiler_params=params(55),
        name="cross",
    )(shard_table, arrived, bottom_out, weights, cross_bias, cotangent)


def spread_sum(value, axis, distances, after=None):
    size = lax.axis_size(axis)
    for distance in distances:
        sent = value.astype(jnp.bfloat16)
        came = lax.ppermute(sent, axis, [(place, place ^ distance) for place in range(size)])
        if after is None:
            value = sent.astype(jnp.float32) + came.astype(jnp.float32)
        else:
            value = add_after(sent, came, after)
    return value


def add_kernel(one_ref, other_ref, after_ref, out_ref):
    out_ref[...] = (one_ref[...].astype(jnp.float32) + other_ref[...].astype(jnp.float32)).astype(jnp.bfloat16)


def add_after(one, other, after):
    vmem = pl.BlockSpec(memory_space=pltpu.VMEM)
    return pl.pallas_call(
        add_kernel,
        in_specs=[vmem, vmem, pl.BlockSpec(memory_space=pl.ANY)],
        out_specs=vmem,
        out_shape=jax.ShapeDtypeStruct(one.shape, jnp.bfloat16),
        compiler_params=params(4),
        name="add_after",
    )(one, other, after)


def hold(value, after):
    anywhere = pl.BlockSpec(memory_space=pl.ANY)

    def kernel(value_ref, after_ref, out_ref):
        pass

    return pl.pallas_call(
        kernel,
        in_specs=[anywhere, anywhere],
        out_specs=anywhere,
        out_shape=jax.ShapeDtypeStruct(value.shape, value.dtype),
        input_output_aliases={0: 0},
        compiler_params=params(4),
        name="hold",
    )(value, after)


def local(
    dense_feats, lookup_ids, lookup_counts, shard_table, embed_tables, first_layer, first_offset, second_layer,
    second_offset, third_layer, third_offset, cross_down, cross_up, cross_bias, cotangent,
):
    examples = dense_feats.shape[0]
    devices = lookup_ids.shape[2] // examples
    weights = lax.all_gather(jnp.concatenate([cross_up, cross_down.T], axis=1), TABLE, axis=0, tiled=True)
    hits, pooled = pool(lookup_ids, lookup_counts, embed_tables)
    pooled = pooled.reshape(devices, examples, pooled.shape[1])
    arrived = lax.all_to_all(pooled, TABLE, split_axis=0, concat_axis=0, tiled=True)
    vmem = pl.BlockSpec(memory_space=pltpu.VMEM)
    bottom_args = (
        dense_feats, first_layer, first_offset[None], second_layer, second_offset[None], third_layer,
        third_offset[None],
    )
    bottom_out = pl.pallas_call(
        bottom_kernel,
        in_specs=[vmem] * 7,
        out_specs=vmem,
        out_shape=jax.ShapeDtypeStruct((examples, WIDTH), jnp.bfloat16),
        compiler_params=params(8),
        name="bottom",
    )(*bottom_args)
    send, bottom_grad, bias_part = cross(shard_table, arrived, bottom_out, weights, cross_bias[None], cotangent)
    returned = lax.all_to_all(send, TABLE, split_axis=0, concat_axis=0, tiled=True)
    parts = lax.axis_size(DP)
    packed = pl.pallas_call(
        bottom_back_kernel,
        in_specs=[vmem] * 9,
        out_specs=vmem,
        out_shape=jax.ShapeDtypeStruct((8 * CHUNK, 128), jnp.bfloat16),
        compiler_params=params(8),
        name="bottom_back",
    )(*bottom_args, bottom_grad, bias_part)
    core, column = lax.axis_index("c"), lax.axis_index("x")
    length = lax.axis_size("x")
    packed = packed.reshape(length, 2, CHUNK, 128)
    theirs = lax.dynamic_index_in_dim(packed, 1 - core, axis=1, keepdims=False)
    came = lax.ppermute(theirs, "c", [(0, 1), (1, 0)])
    mine = lax.dynamic_index_in_dim(packed, core, axis=1, keepdims=False)
    both = mine.astype(jnp.float32) + came.astype(jnp.float32)
    part = lax.dynamic_index_in_dim(both, column, axis=0, keepdims=False)
    narrow = both.astype(jnp.bfloat16)
    for shift in range(1, length):
        piece = lax.dynamic_index_in_dim(narrow, (column + shift) % length, axis=0, keepdims=False)
        piece = lax.ppermute(piece, "x", [(place, (place + shift) % length) for place in range(length)])
        part = part + piece.astype(jnp.float32)
    part = spread_sum(part, "zl", (1,), returned)
    group = ("zh", "yl")
    part = jnp.broadcast_to(part.astype(jnp.bfloat16), (lax.axis_size(group), CHUNK, 128))
    part = lax.all_to_all(part, group, split_axis=0, concat_axis=0, tiled=True)
    part = jnp.sum(part.astype(jnp.float32), axis=0)

    table_parts = table_grads(hits, returned.reshape(-1, returned.shape[2]), parts)
    table_parts = hold(table_parts, part)
    table_parts = lax.all_to_all(table_parts, DP, split_axis=0, concat_axis=0, tiled=True)
    table_grad = jnp.sum(table_parts.astype(jnp.float32), axis=0)

    part = spread_sum(part, "yh", (1, 2)).astype(jnp.bfloat16)
    other = lax.ppermute(part, "c", [(0, 1), (1, 0)])
    pair = jnp.where(core == 0, jnp.stack([part, other]), jnp.stack([other, part]))
    whole = lax.all_gather(pair.reshape(2 * CHUNK, 128), "x", axis=0, tiled=True)
    first_grad, second_grad, third_grad, first_sum, second_sum, third_sum, bias_sum = pl.pallas_call(
        unpack_kernel,
        in_specs=[vmem],
        out_specs=[vmem] * 7,
        out_shape=[
            jax.ShapeDtypeStruct(shape, jnp.float32)
            for shape in (
                first_layer.shape, second_layer.shape, third_layer.shape, (1, first_layer.shape[1]),
                (1, second_layer.shape[1]), (1, third_layer.shape[1]), (1, cross_bias.shape[0]),
            )
        ],
        compiler_params=params(8),
        name="unpack",
    )(whole)
    return (
        table_grad, first_grad, first_sum[0], second_grad, second_sum[0], third_grad, third_sum[0], bias_sum[0],
    )


def solution(mesh):
    fine = Mesh(mesh.devices.reshape(4, 4, 2, 4, 2, 2), EVERY)
    placed = (
        P(EVERY, None),
        P(TABLE, None, DP),
        P(TABLE, DP),
        P(),
        P(TABLE, None, None),
        P(),
        P(),
        P(),
        P(),
        P(),
        P(),
        P(None, TABLE),
        P(TABLE, None),
        P(),
        P(EVERY, None),
    )
    return jax.shard_map(
        local,
        mesh=fine,
        in_specs=placed,
        out_specs=(P(TABLE, DP, None), P(), P(), P(), P(), P(), P(), P()),
        check_vma=False,
    )
```

```python
import math

import jax
import jax.numpy as jnp
from jax import lax
from jax.experimental import pallas as pl
from jax.experimental.pallas import tpu as pltpu
from jax.sharding import Mesh
from jax.sharding import PartitionSpec as P

TABLES = 26
WIDTH = 128
GROUP = 32
BLOCK = 256
LOW = 256
TABLE = ("yh", "yl", "c")
DP = ("x", "zh", "zl")
EVERY = ("x", "zh", "zl", "yh", "yl", "c")
CHUNK = 176

NT = (((1,), (1,)), ((), ()))
TN = (((0,), (0,)), ((), ()))


def dot(a, b, dims=(((1,), (0,)), ((), ()))):
    return lax.dot_general(a, b, dims, preferred_element_type=jnp.float32)


def params(megabytes):
    return pltpu.CompilerParams(vmem_limit_bytes=megabytes * 1024 * 1024)


def pool_kernel(code_ref, table_ref, hits_ref, pooled_ref):
    slots = code_ref.shape[2]
    rows = table_ref.shape[1]
    lane = lax.broadcasted_iota(jnp.int32, (GROUP, slots), 1)
    own = (lane & (GROUP - 1)) == lax.broadcasted_iota(jnp.int32, (GROUP, slots), 0)
    low_iota = lax.broadcasted_iota(jnp.int32, (LOW, slots), 0).astype(jnp.float32).astype(jnp.bfloat16)
    one = jnp.ones((), jnp.bfloat16)
    zero = jnp.zeros((), jnp.bfloat16)
    for group in range(BLOCK // GROUP):
        code = code_ref[0, pl.ds(group, 1), :]
        high = jnp.broadcast_to(code >> 8, (GROUP, slots))
        high = jnp.where(own, high, -1).astype(jnp.float32).astype(jnp.bfloat16)
        low = (code & (LOW - 1)).astype(jnp.float32).astype(jnp.bfloat16)
        right = jnp.where(low_iota == jnp.broadcast_to(low, (LOW, slots)), one, zero)
        left = jnp.concatenate(
            [jnp.where(high == jnp.full((), part, jnp.bfloat16), one, zero) for part in range(rows // LOW)], axis=0
        )
        hits = dot(left, right, NT).astype(jnp.bfloat16)
        for part in range(rows // LOW):
            hits_ref[0, part, pl.ds(group * GROUP, GROUP), :] = hits[part * GROUP : (part + 1) * GROUP]
    total = dot(hits_ref[0, 0], table_ref[0, 0:LOW])
    for part in range(1, rows // LOW):
        total = total + dot(hits_ref[0, part], table_ref[0, part * LOW : part * LOW + LOW])
    pooled_ref[...] = total.astype(jnp.bfloat16)


def pool(lookup_ids, lookup_counts, embed_tables):
    shards, hot, batch = lookup_ids.shape
    rows = embed_tables.shape[1]
    slot = lax.broadcasted_iota(jnp.int32, lookup_ids.shape, 1)
    code = jnp.where(lookup_counts[:, None, :] > slot, lookup_ids, -1)
    code = code.reshape(shards, hot, batch // GROUP, GROUP).transpose(0, 2, 1, 3)
    code = code.reshape(shards, batch // GROUP, hot * GROUP)
    return pl.pallas_call(
        pool_kernel,
        grid=(shards, batch // BLOCK),
        in_specs=[
            pl.BlockSpec((1, BLOCK // GROUP, hot * GROUP), lambda s, b: (s, b, 0)),
            pl.BlockSpec((1, rows, WIDTH), lambda s, b: (s, 0, 0)),
        ],
        out_specs=[
            pl.BlockSpec((1, rows // LOW, BLOCK, LOW), lambda s, b: (s, 0, b, 0)),
            pl.BlockSpec((BLOCK, WIDTH), lambda s, b: (b, s)),
        ],
        out_shape=[
            pltpu.HBM((shards, rows // LOW, batch, LOW), jnp.bfloat16),
            jax.ShapeDtypeStruct((batch, shards * WIDTH), jnp.bfloat16),
        ],
        compiler_params=params(8),
        name="pool",
    )(code, embed_tables)


def table_grad_kernel(hits_ref, grad_ref, out_ref, turned):
    @pl.when(pl.program_id(1) == 0)
    def _():
        turned[...] = grad_ref[...].T

    blocks = hits_ref.shape[1]
    step = out_ref.shape[0] // blocks
    for block in range(blocks):
        total = dot(turned[...], hits_ref[0, block]).T.astype(jnp.bfloat16)
        out_ref[block * step : block * step + step] = total.reshape(step, *out_ref.shape[1:])


def table_grads(hits, grads, parts):
    shards, blocks, batch, low = hits.shape
    each = blocks * low // parts
    wide = math.gcd(blocks, 4)
    step = wide * low // each
    return pl.pallas_call(
        table_grad_kernel,
        grid=(shards, blocks // wide),
        in_specs=[
            pl.BlockSpec((1, wide, batch, low), lambda s, r: (s, r, 0, 0)),
            pl.BlockSpec((batch, WIDTH), lambda s, r: (0, s)),
        ],
        out_specs=pl.BlockSpec((step, 1, each, WIDTH), lambda s, r: (r, s, 0, 0)),
        out_shape=jax.ShapeDtypeStruct((parts, shards, each, WIDTH), jnp.bfloat16),
        scratch_shapes=[pltpu.VMEM((WIDTH, batch), jnp.bfloat16)],
        compiler_params=params(46),
        cost_estimate=pl.CostEstimate(
            flops=2 * shards * batch * blocks * low * WIDTH,
            bytes_accessed=2 * shards * batch * (blocks * low + 2 * WIDTH),
            transcendentals=0,
        ),
        name="table_grads",
    )(hits, grads)


def silu(value):
    return value / (1.0 + jnp.exp(-value))


def silu_slope(value):
    sigmoid = 1.0 / (1.0 + jnp.exp(-value))
    return sigmoid * (1.0 + value * (1.0 - sigmoid))


def bottom_pre(dense, w1, b1, w2, b2, w3, b3):
    first_pre = dot(dense[...], w1[...]) + b1[...]
    first_act = silu(first_pre).astype(jnp.bfloat16)
    second_pre = dot(first_act, w2[...]) + b2[...]
    second_act = silu(second_pre).astype(jnp.bfloat16)
    third_pre = dot(second_act, w3[...]) + b3[...]
    return first_pre, first_act, second_pre, second_act, third_pre


def bottom_kernel(dense, w1, b1, w2, b2, w3, b3, out_ref):
    out_ref[...] = silu(bottom_pre(dense, w1, b1, w2, b2, w3, b3)[4]).astype(jnp.bfloat16)


def bottom_back_kernel(dense, w1, b1, w2, b2, w3, b3, grad_ref, bias_ref, out_ref):
    first_pre, first_act, second_pre, second_act, third_pre = bottom_pre(dense, w1, b1, w2, b2, w3, b3)
    third_delta = silu_slope(third_pre) * grad_ref[...].astype(jnp.float32)
    third_delta = third_delta.astype(jnp.bfloat16)
    out_ref[1024:1280, :] = dot(second_act, third_delta, TN).astype(jnp.bfloat16)
    second_delta = (silu_slope(second_pre) * dot(third_delta, w3[...], NT)).astype(jnp.bfloat16)
    second_grad = dot(first_act, second_delta, TN).astype(jnp.bfloat16)
    out_ref[0:512, :] = second_grad[:, :128]
    out_ref[512:1024, :] = second_grad[:, 128:]
    first_delta = (silu_slope(first_pre) * dot(second_delta, w2[...], NT)).astype(jnp.bfloat16)
    first_grad = dot(dense[...], first_delta, TN)
    first_grad = jnp.concatenate([first_grad, jnp.zeros((3, first_grad.shape[1]), jnp.float32)], axis=0)
    for part in range(4):
        out_ref[1280 + 16 * part : 1296 + 16 * part, :] = first_grad[:, part * 128 : part * 128 + 128].astype(
            jnp.bfloat16
        )
    first_sum = jnp.sum(first_delta.astype(jnp.float32), axis=0, keepdims=True)
    second_sum = jnp.sum(second_delta.astype(jnp.float32), axis=0, keepdims=True)
    third_sum = jnp.sum(third_delta.astype(jnp.float32), axis=0, keepdims=True)
    rows = [first_sum[:, part * 128 : part * 128 + 128] for part in range(4)]
    rows += [second_sum[:, part * 128 : part * 128 + 128] for part in range(2)]
    rows += [third_sum, jnp.zeros((9, 128), jnp.float32)]
    out_ref[1344:1360, :] = jnp.concatenate(rows, axis=0).astype(jnp.bfloat16)
    out_ref[1360:1392, :] = bias_ref[...].astype(jnp.bfloat16)
    out_ref[1392:1408, :] = jnp.zeros((16, 128), jnp.bfloat16)


def unpack_kernel(whole, first_grad, second_grad, third_grad, first_sum, second_sum, third_sum, bias_sum):
    second_grad[:, 0:128] = whole[0:512].astype(jnp.float32)
    second_grad[:, 128:256] = whole[512:1024].astype(jnp.float32)
    third_grad[...] = whole[1024:1280].astype(jnp.float32)
    for part in range(4):
        block = whole[1280 + 16 * part : 1296 + 16 * part].astype(jnp.float32)
        first_grad[:, part * 128 : part * 128 + 128] = block[0:13]
    sums = whole[1344:1360].astype(jnp.float32)
    for part in range(4):
        first_sum[:, part * 128 : part * 128 + 128] = sums[part : part + 1]
    for part in range(2):
        second_sum[:, part * 128 : part * 128 + 128] = sums[4 + part : 5 + part]
    third_sum[...] = sums[6:7]
    biases = whole[1360:1392].astype(jnp.float32)
    for part in range(27):
        bias_sum[:, part * 128 : part * 128 + 128] = biases[part : part + 1]


def mix_kernel(owner_ref, arrived_ref, bottom_ref, cot_ref, inputs, mixed, bias_grad_ref, total):
    blocks = total.shape[0]
    total[1:] = jnp.zeros_like(total[1:])
    total[0] = bottom_ref[...].astype(jnp.float32)
    for shard in range(owner_ref.shape[0]):
        place = owner_ref[shard] + 1
        piece = arrived_ref[shard // 2, :, (shard % 2) * WIDTH : (shard % 2) * WIDTH + WIDTH]
        total[place] = total[place] + piece.astype(jnp.float32)
    bias_grad_ref[...] = jnp.zeros_like(bias_grad_ref)
    for block in range(blocks):
        columns = slice(block * WIDTH, block * WIDTH + WIDTH)
        piece = total[block].astype(jnp.bfloat16)
        inputs[:, columns] = piece
        mix_grad = cot_ref[:, columns].astype(jnp.float32) * piece.astype(jnp.float32)
        mixed[:, columns] = mix_grad.astype(jnp.bfloat16)
        bias_grad_ref[block : block + 1, :] = jnp.sum(mix_grad, axis=0, keepdims=True)


def cross_kernel(
    owner_ref, inputs, mixed, weights_ref, bias_ref, cot_ref, send_ref, bottom_grad_ref, grads, up, down, low_rank,
    rank_grad, landed,
):
    wide = inputs.shape[1]
    shards = owner_ref.shape[0]
    parts = landed.shape[0] // 2
    ranks = up.shape[0] // parts
    copies = []
    for part in range(parts):
        rows = pl.ds(part * ranks, ranks)
        for place, (held, first) in enumerate(((down, wide), (up, 0))):
            copy = pltpu.make_async_copy(
                weights_ref.at[rows, first : first + wide], held.at[rows, :], landed.at[part * 2 + place]
            )
            copy.start()
            copies.append(copy)
    for part in range(parts):
        rows = slice(part * ranks, part * ranks + ranks)
        copies[2 * part].wait()
        low_rank[:, rows] = dot(inputs[...], down[rows, :], NT).astype(jnp.bfloat16)
        copies[2 * part + 1].wait()
        rank_grad[:, rows] = dot(mixed[...], up[rows, :], NT).astype(jnp.bfloat16)
    step = 3 * WIDTH
    for part in range(wide // step):
        columns = slice(part * step, part * step + step)
        mixing = dot(low_rank[...], up[:, columns]) + bias_ref[:, columns]
        back = dot(rank_grad[...], down[:, columns])
        grad = (cot_ref[:, columns].astype(jnp.float32) * (mixing + 1.0) + back).astype(jnp.bfloat16)
        for inner in range(3):
            grads[part * 3 + inner] = grad[:, inner * WIDTH : inner * WIDTH + WIDTH]
    bottom_grad_ref[...] = grads[0]
    for shard in range(shards):
        send_ref[shard // 2, :, (shard % 2) * WIDTH : (shard % 2) * WIDTH + WIDTH] = grads[owner_ref[shard] + 1]


def cross(shard_table, arrived, bottom_out, weights, cross_bias, cotangent):
    examples, wide = cotangent.shape
    blocks = wide // WIDTH
    ranks = weights.shape[0]
    vmem = pl.BlockSpec(memory_space=pltpu.VMEM)
    smem = pl.BlockSpec(memory_space=pltpu.SMEM)
    inputs, mixed, bias_part = pl.pallas_call(
        mix_kernel,
        in_specs=[smem] + [vmem] * 3,
        out_specs=[vmem] * 3,
        out_shape=[
            jax.ShapeDtypeStruct((examples, wide), jnp.bfloat16),
            jax.ShapeDtypeStruct((examples, wide), jnp.bfloat16),
            jax.ShapeDtypeStruct((32, WIDTH), jnp.float32),
        ],
        scratch_shapes=[pltpu.VMEM((blocks, examples, WIDTH), jnp.float32)],
        compiler_params=params(16),
        name="mix",
    )(shard_table, arrived, bottom_out, cotangent)
    send, bottom_grad = pl.pallas_call(
        cross_kernel,
        in_specs=[smem, vmem, vmem, pl.BlockSpec(memory_space=pltpu.HBM), vmem, vmem],
        out_specs=[vmem] * 2,
        out_shape=[
            jax.ShapeDtypeStruct(arrived.shape, jnp.bfloat16),
            jax.ShapeDtypeStruct((examples, WIDTH), jnp.bfloat16),
        ],
        scratch_shapes=[
            pltpu.VMEM((blocks, examples, WIDTH), jnp.bfloat16),
            pltpu.VMEM((ranks, wide), jnp.bfloat16),
            pltpu.VMEM((ranks, wide), jnp.bfloat16),
            pltpu.VMEM((examples, ranks), jnp.bfloat16),
            pltpu.VMEM((examples, ranks), jnp.bfloat16),
            pltpu.SemaphoreType.DMA((4,)),
        ],
        compiler_params=params(50),
        name="cross",
    )(shard_table, inputs, mixed, weights, cross_bias, cotangent)
    return send, bottom_grad, bias_part


def spread_sum(value, axis, distances, after=None):
    size = lax.axis_size(axis)
    for distance in distances:
        sent = value.astype(jnp.bfloat16)
        came = lax.ppermute(sent, axis, [(place, place ^ distance) for place in range(size)])
        if after is None:
            value = sent.astype(jnp.float32) + came.astype(jnp.float32)
        else:
            value = add_after(sent, came, after)
    return value


def add_kernel(one_ref, other_ref, after_ref, out_ref):
    out_ref[...] = (one_ref[...].astype(jnp.float32) + other_ref[...].astype(jnp.float32)).astype(jnp.bfloat16)


def add_after(one, other, after):
    vmem = pl.BlockSpec(memory_space=pltpu.VMEM)
    return pl.pallas_call(
        add_kernel,
        in_specs=[vmem, vmem, pl.BlockSpec(memory_space=pl.ANY)],
        out_specs=vmem,
        out_shape=jax.ShapeDtypeStruct(one.shape, jnp.bfloat16),
        compiler_params=params(4),
        name="add_after",
    )(one, other, after)


def hold(value, after):
    anywhere = pl.BlockSpec(memory_space=pl.ANY)

    def kernel(value_ref, after_ref, out_ref):
        pass

    return pl.pallas_call(
        kernel,
        in_specs=[anywhere, anywhere],
        out_specs=anywhere,
        out_shape=jax.ShapeDtypeStruct(value.shape, value.dtype),
        input_output_aliases={0: 0},
        compiler_params=params(4),
        name="hold",
    )(value, after)


def local(
    dense_feats, lookup_ids, lookup_counts, shard_table, embed_tables, first_layer, first_offset, second_layer,
    second_offset, third_layer, third_offset, cross_down, cross_up, cross_bias, cotangent,
):
    examples = dense_feats.shape[0]
    devices = lookup_ids.shape[2] // examples
    weights = lax.all_gather(jnp.concatenate([cross_up, cross_down.T], axis=1), TABLE, axis=0, tiled=True)
    hits, pooled = pool(lookup_ids, lookup_counts, embed_tables)
    pooled = pooled.reshape(devices, examples, pooled.shape[1])
    arrived = lax.all_to_all(pooled, TABLE, split_axis=0, concat_axis=0, tiled=True)
    vmem = pl.BlockSpec(memory_space=pltpu.VMEM)
    bottom_args = (
        dense_feats, first_layer, first_offset[None], second_layer, second_offset[None], third_layer,
        third_offset[None],
    )
    bottom_out = pl.pallas_call(
        bottom_kernel,
        in_specs=[vmem] * 7,
        out_specs=vmem,
        out_shape=jax.ShapeDtypeStruct((examples, WIDTH), jnp.bfloat16),
        compiler_params=params(8),
        name="bottom",
    )(*bottom_args)
    send, bottom_grad, bias_part = cross(shard_table, arrived, bottom_out, weights, cross_bias[None], cotangent)
    returned = lax.all_to_all(send, TABLE, split_axis=0, concat_axis=0, tiled=True)
    parts = lax.axis_size(DP)
    packed = pl.pallas_call(
        bottom_back_kernel,
        in_specs=[vmem] * 9,
        out_specs=vmem,
        out_shape=jax.ShapeDtypeStruct((8 * CHUNK, 128), jnp.bfloat16),
        compiler_params=params(8),
        name="bottom_back",
    )(*bottom_args, bottom_grad, bias_part)
    core, column = lax.axis_index("c"), lax.axis_index("x")
    length = lax.axis_size("x")
    packed = packed.reshape(length, 2, CHUNK, 128)
    theirs = lax.dynamic_index_in_dim(packed, 1 - core, axis=1, keepdims=False)
    came = lax.ppermute(theirs, "c", [(0, 1), (1, 0)])
    mine = lax.dynamic_index_in_dim(packed, core, axis=1, keepdims=False)
    both = mine.astype(jnp.float32) + came.astype(jnp.float32)
    part = lax.dynamic_index_in_dim(both, column, axis=0, keepdims=False)
    narrow = both.astype(jnp.bfloat16)
    for shift in range(1, length):
        piece = lax.dynamic_index_in_dim(narrow, (column + shift) % length, axis=0, keepdims=False)
        piece = lax.ppermute(piece, "x", [(place, (place + shift) % length) for place in range(length)])
        part = part + piece.astype(jnp.float32)
    part = spread_sum(part, "zl", (1,), returned)
    group = ("zh", "yl")
    part = jnp.broadcast_to(part.astype(jnp.bfloat16), (lax.axis_size(group), CHUNK, 128))
    part = lax.all_to_all(part, group, split_axis=0, concat_axis=0, tiled=True)
    part = jnp.sum(part.astype(jnp.float32), axis=0)

    table_parts = table_grads(hits, returned.reshape(-1, returned.shape[2]), parts)
    table_parts = hold(table_parts, part)
    table_parts = lax.all_to_all(table_parts, DP, split_axis=0, concat_axis=0, tiled=True)
    table_grad = jnp.sum(table_parts.astype(jnp.float32), axis=0)

    part = spread_sum(part, "yh", (1, 2)).astype(jnp.bfloat16)
    other = lax.ppermute(part, "c", [(0, 1), (1, 0)])
    pair = jnp.where(core == 0, jnp.stack([part, other]), jnp.stack([other, part]))
    whole = lax.all_gather(pair.reshape(2 * CHUNK, 128), "x", axis=0, tiled=True)
    first_grad, second_grad, third_grad, first_sum, second_sum, third_sum, bias_sum = pl.pallas_call(
        unpack_kernel,
        in_specs=[vmem],
        out_specs=[vmem] * 7,
        out_shape=[
            jax.ShapeDtypeStruct(shape, jnp.float32)
            for shape in (
                first_layer.shape, second_layer.shape, third_layer.shape, (1, first_layer.shape[1]),
                (1, second_layer.shape[1]), (1, third_layer.shape[1]), (1, cross_bias.shape[0]),
            )
        ],
        compiler_params=params(8),
        name="unpack",
    )(whole)
    return (
        table_grad, first_grad, first_sum[0], second_grad, second_sum[0], third_grad, third_sum[0], bias_sum[0],
    )


def solution(mesh):
    fine = Mesh(mesh.devices.reshape(4, 4, 2, 4, 2, 2), EVERY)
    placed = (
        P(EVERY, None),
        P(TABLE, None, DP),
        P(TABLE, DP),
        P(),
        P(TABLE, None, None),
        P(),
        P(),
        P(),
        P(),
        P(),
        P(),
        P(None, TABLE),
        P(TABLE, None),
        P(),
        P(EVERY, None),
    )
    return jax.shard_map(
        local,
        mesh=fine,
        in_specs=placed,
        out_specs=(P(TABLE, DP, None), P(), P(), P(), P(), P(), P(), P()),
        check_vma=False,
    )
```

```python
import math

import jax
import jax.numpy as jnp
from jax import lax
from jax.experimental import pallas as pl
from jax.experimental.pallas import tpu as pltpu
from jax.sharding import Mesh
from jax.sharding import PartitionSpec as P

TABLES = 26
WIDTH = 128
GROUP = 32
BLOCK = 256
LOW = 256
TABLE = ("yh", "yl", "c")
DP = ("x", "zh", "zl")
EVERY = ("x", "zh", "zl", "yh", "yl", "c")
CHUNK = 176

NT = (((1,), (1,)), ((), ()))
TN = (((0,), (0,)), ((), ()))


def dot(a, b, dims=(((1,), (0,)), ((), ()))):
    return lax.dot_general(a, b, dims, preferred_element_type=jnp.float32)


def params(megabytes):
    return pltpu.CompilerParams(vmem_limit_bytes=megabytes * 1024 * 1024)


def pool_kernel(code_ref, table_ref, hits_ref, pooled_ref):
    slots = code_ref.shape[2]
    rows = table_ref.shape[1]
    lane = lax.broadcasted_iota(jnp.int32, (GROUP, slots), 1)
    own = (lane & (GROUP - 1)) == lax.broadcasted_iota(jnp.int32, (GROUP, slots), 0)
    low_iota = lax.broadcasted_iota(jnp.int32, (LOW, slots), 0).astype(jnp.float32).astype(jnp.bfloat16)
    one = jnp.ones((), jnp.bfloat16)
    zero = jnp.zeros((), jnp.bfloat16)
    for group in range(BLOCK // GROUP):
        code = code_ref[0, pl.ds(group, 1), :]
        high = jnp.broadcast_to(code >> 8, (GROUP, slots))
        high = jnp.where(own, high, -1).astype(jnp.float32).astype(jnp.bfloat16)
        low = (code & (LOW - 1)).astype(jnp.float32).astype(jnp.bfloat16)
        right = jnp.where(low_iota == jnp.broadcast_to(low, (LOW, slots)), one, zero)
        left = jnp.concatenate(
            [jnp.where(high == jnp.full((), part, jnp.bfloat16), one, zero) for part in range(rows // LOW)], axis=0
        )
        hits = dot(left, right, NT).astype(jnp.bfloat16)
        for part in range(rows // LOW):
            hits_ref[0, part, pl.ds(group * GROUP, GROUP), :] = hits[part * GROUP : (part + 1) * GROUP]
    total = dot(hits_ref[0, 0], table_ref[0, 0:LOW])
    for part in range(1, rows // LOW):
        total = total + dot(hits_ref[0, part], table_ref[0, part * LOW : part * LOW + LOW])
    pooled_ref[...] = total.astype(jnp.bfloat16)


def pool(lookup_ids, lookup_counts, embed_tables):
    shards, hot, batch = lookup_ids.shape
    rows = embed_tables.shape[1]
    slot = lax.broadcasted_iota(jnp.int32, lookup_ids.shape, 1)
    code = jnp.where(lookup_counts[:, None, :] > slot, lookup_ids, -1)
    code = code.reshape(shards, hot, batch // GROUP, GROUP).transpose(0, 2, 1, 3)
    code = code.reshape(shards, batch // GROUP, hot * GROUP)
    return pl.pallas_call(
        pool_kernel,
        grid=(shards, batch // BLOCK),
        in_specs=[
            pl.BlockSpec((1, BLOCK // GROUP, hot * GROUP), lambda s, b: (s, b, 0)),
            pl.BlockSpec((1, rows, WIDTH), lambda s, b: (s, 0, 0)),
        ],
        out_specs=[
            pl.BlockSpec((1, rows // LOW, BLOCK, LOW), lambda s, b: (s, 0, b, 0)),
            pl.BlockSpec((BLOCK, WIDTH), lambda s, b: (b, s)),
        ],
        out_shape=[
            pltpu.HBM((shards, rows // LOW, batch, LOW), jnp.bfloat16),
            jax.ShapeDtypeStruct((batch, shards * WIDTH), jnp.bfloat16),
        ],
        compiler_params=params(8),
        name="pool",
    )(code, embed_tables)


def table_grad_kernel(hits_ref, grad_ref, out_ref, turned):
    @pl.when(pl.program_id(1) == 0)
    def _():
        turned[...] = grad_ref[...].T

    blocks = hits_ref.shape[1]
    step = out_ref.shape[0] // blocks
    for block in range(blocks):
        total = dot(turned[...], hits_ref[0, block]).T.astype(jnp.bfloat16)
        out_ref[block * step : block * step + step] = total.reshape(step, *out_ref.shape[1:])


def table_grads(hits, grads, parts):
    shards, blocks, batch, low = hits.shape
    each = blocks * low // parts
    wide = math.gcd(blocks, 4)
    step = wide * low // each
    return pl.pallas_call(
        table_grad_kernel,
        grid=(shards, blocks // wide),
        in_specs=[
            pl.BlockSpec((1, wide, batch, low), lambda s, r: (s, r, 0, 0)),
            pl.BlockSpec((batch, WIDTH), lambda s, r: (0, s)),
        ],
        out_specs=pl.BlockSpec((step, 1, each, WIDTH), lambda s, r: (r, s, 0, 0)),
        out_shape=jax.ShapeDtypeStruct((parts, shards, each, WIDTH), jnp.bfloat16),
        scratch_shapes=[pltpu.VMEM((WIDTH, batch), jnp.bfloat16)],
        compiler_params=params(46),
        cost_estimate=pl.CostEstimate(
            flops=2 * shards * batch * blocks * low * WIDTH,
            bytes_accessed=2 * shards * batch * (blocks * low + 2 * WIDTH),
            transcendentals=0,
        ),
        name="table_grads",
    )(hits, grads)


def silu(value):
    return value / (1.0 + jnp.exp(-value))


def silu_slope(value):
    sigmoid = 1.0 / (1.0 + jnp.exp(-value))
    return sigmoid * (1.0 + value * (1.0 - sigmoid))


def bottom_pre(dense, w1, b1, w2, b2, w3, b3):
    first_pre = dot(dense[...], w1[...]) + b1[...]
    first_act = silu(first_pre).astype(jnp.bfloat16)
    second_pre = dot(first_act, w2[...]) + b2[...]
    second_act = silu(second_pre).astype(jnp.bfloat16)
    third_pre = dot(second_act, w3[...]) + b3[...]
    return first_pre, first_act, second_pre, second_act, third_pre


def bottom_kernel(dense, w1, b1, w2, b2, w3, b3, out_ref):
    out_ref[...] = silu(bottom_pre(dense, w1, b1, w2, b2, w3, b3)[4]).astype(jnp.bfloat16)


def bottom_back_kernel(dense, w1, b1, w2, b2, w3, b3, grad_ref, bias_ref, out_ref):
    first_pre, first_act, second_pre, second_act, third_pre = bottom_pre(dense, w1, b1, w2, b2, w3, b3)
    third_delta = silu_slope(third_pre) * grad_ref[...].astype(jnp.float32)
    third_delta = third_delta.astype(jnp.bfloat16)
    out_ref[1024:1280, :] = dot(second_act, third_delta, TN).astype(jnp.bfloat16)
    second_delta = (silu_slope(second_pre) * dot(third_delta, w3[...], NT)).astype(jnp.bfloat16)
    second_grad = dot(first_act, second_delta, TN).astype(jnp.bfloat16)
    out_ref[0:512, :] = second_grad[:, :128]
    out_ref[512:1024, :] = second_grad[:, 128:]
    first_delta = (silu_slope(first_pre) * dot(second_delta, w2[...], NT)).astype(jnp.bfloat16)
    first_grad = dot(dense[...], first_delta, TN)
    first_grad = jnp.concatenate([first_grad, jnp.zeros((3, first_grad.shape[1]), jnp.float32)], axis=0)
    for part in range(4):
        out_ref[1280 + 16 * part : 1296 + 16 * part, :] = first_grad[:, part * 128 : part * 128 + 128].astype(
            jnp.bfloat16
        )
    first_sum = jnp.sum(first_delta.astype(jnp.float32), axis=0, keepdims=True)
    second_sum = jnp.sum(second_delta.astype(jnp.float32), axis=0, keepdims=True)
    third_sum = jnp.sum(third_delta.astype(jnp.float32), axis=0, keepdims=True)
    rows = [first_sum[:, part * 128 : part * 128 + 128] for part in range(4)]
    rows += [second_sum[:, part * 128 : part * 128 + 128] for part in range(2)]
    rows += [third_sum, jnp.zeros((9, 128), jnp.float32)]
    out_ref[1344:1360, :] = jnp.concatenate(rows, axis=0).astype(jnp.bfloat16)
    out_ref[1360:1392, :] = bias_ref[...].astype(jnp.bfloat16)
    out_ref[1392:1408, :] = jnp.zeros((16, 128), jnp.bfloat16)


def unpack_kernel(whole, first_grad, second_grad, third_grad, first_sum, second_sum, third_sum, bias_sum):
    second_grad[:, 0:128] = whole[0:512].astype(jnp.float32)
    second_grad[:, 128:256] = whole[512:1024].astype(jnp.float32)
    third_grad[...] = whole[1024:1280].astype(jnp.float32)
    for part in range(4):
        block = whole[1280 + 16 * part : 1296 + 16 * part].astype(jnp.float32)
        first_grad[:, part * 128 : part * 128 + 128] = block[0:13]
    sums = whole[1344:1360].astype(jnp.float32)
    for part in range(4):
        first_sum[:, part * 128 : part * 128 + 128] = sums[part : part + 1]
    for part in range(2):
        second_sum[:, part * 128 : part * 128 + 128] = sums[4 + part : 5 + part]
    third_sum[...] = sums[6:7]
    biases = whole[1360:1392].astype(jnp.float32)
    for part in range(27):
        bias_sum[:, part * 128 : part * 128 + 128] = biases[part : part + 1]


def cross_kernel(
    owner_ref, arrived_ref, bottom_ref, weights_ref, bias_ref, cot_ref,
    send_ref, bottom_grad_ref, bias_grad_ref, total, inputs, mixed, grads, up, down, arrived_at,
):
    blocks = total.shape[0]
    wide = blocks * WIDTH
    shards = owner_ref.shape[0]
    fetch_down = pltpu.make_async_copy(weights_ref.at[:, wide : 2 * wide], down, arrived_at.at[0])
    fetch_up = pltpu.make_async_copy(weights_ref.at[:, 0:wide], up, arrived_at.at[1])
    fetch_down.start()
    fetch_up.start()
    total[1:] = jnp.zeros_like(total[1:])
    total[0] = bottom_ref[...].astype(jnp.float32)
    for shard in range(shards):
        place = owner_ref[shard] + 1
        piece = arrived_ref[shard // 2, :, (shard % 2) * WIDTH : (shard % 2) * WIDTH + WIDTH]
        total[place] = total[place] + piece.astype(jnp.float32)
    bias_grad_ref[...] = jnp.zeros_like(bias_grad_ref)
    for block in range(blocks):
        columns = slice(block * WIDTH, block * WIDTH + WIDTH)
        piece = total[block].astype(jnp.bfloat16)
        inputs[:, columns] = piece
        mix_grad = cot_ref[:, columns].astype(jnp.float32) * piece.astype(jnp.float32)
        mixed[:, columns] = mix_grad.astype(jnp.bfloat16)
        bias_grad_ref[block : block + 1, :] = jnp.sum(mix_grad, axis=0, keepdims=True)
    fetch_down.wait()
    low_rank = dot(inputs[...], down[...], NT).astype(jnp.bfloat16)
    fetch_up.wait()
    rank_grad = dot(mixed[...], up[...], NT).astype(jnp.bfloat16)
    step = 3 * WIDTH
    for part in range(wide // step):
        columns = slice(part * step, part * step + step)
        mixing = dot(low_rank, up[:, columns]) + bias_ref[:, columns]
        back = dot(rank_grad, down[:, columns])
        grad = (cot_ref[:, columns].astype(jnp.float32) * (mixing + 1.0) + back).astype(jnp.bfloat16)
        for inner in range(3):
            grads[part * 3 + inner] = grad[:, inner * WIDTH : inner * WIDTH + WIDTH]
    bottom_grad_ref[...] = grads[0]
    for shard in range(shards):
        send_ref[shard // 2, :, (shard % 2) * WIDTH : (shard % 2) * WIDTH + WIDTH] = grads[owner_ref[shard] + 1]


def cross(shard_table, arrived, bottom_out, weights, cross_bias, cotangent):
    examples, wide = cotangent.shape
    blocks = wide // WIDTH
    vmem = pl.BlockSpec(memory_space=pltpu.VMEM)
    return pl.pallas_call(
        cross_kernel,
        in_specs=[pl.BlockSpec(memory_space=pltpu.SMEM), vmem, vmem, pl.BlockSpec(memory_space=pltpu.HBM), vmem, vmem],
        out_specs=[vmem] * 3,
        out_shape=[
            jax.ShapeDtypeStruct(arrived.shape, jnp.bfloat16),
            jax.ShapeDtypeStruct((examples, WIDTH), jnp.bfloat16),
            jax.ShapeDtypeStruct((32, WIDTH), jnp.float32),
        ],
        scratch_shapes=[
            pltpu.VMEM((blocks, examples, WIDTH), jnp.float32),
            pltpu.VMEM((examples, wide), jnp.bfloat16),
            pltpu.VMEM((examples, wide), jnp.bfloat16),
            pltpu.VMEM((blocks, examples, WIDTH), jnp.bfloat16),
            pltpu.VMEM((weights.shape[0], wide), jnp.bfloat16),
            pltpu.VMEM((weights.shape[0], wide), jnp.bfloat16),
            pltpu.SemaphoreType.DMA((2,)),
        ],
        compiler_params=params(55),
        name="cross",
    )(shard_table, arrived, bottom_out, weights, cross_bias, cotangent)


def spread_sum(value, axis, distances, after=None):
    size = lax.axis_size(axis)
    for distance in distances:
        sent = value.astype(jnp.bfloat16)
        came = lax.ppermute(sent, axis, [(place, place ^ distance) for place in range(size)])
        if after is None:
            value = sent.astype(jnp.float32) + came.astype(jnp.float32)
        else:
            value = add_after(sent, came, after)
    return value


def add_kernel(one_ref, other_ref, after_ref, out_ref):
    out_ref[...] = (one_ref[...].astype(jnp.float32) + other_ref[...].astype(jnp.float32)).astype(jnp.bfloat16)


def add_after(one, other, after):
    vmem = pl.BlockSpec(memory_space=pltpu.VMEM)
    return pl.pallas_call(
        add_kernel,
        in_specs=[vmem, vmem, pl.BlockSpec(memory_space=pl.ANY)],
        out_specs=vmem,
        out_shape=jax.ShapeDtypeStruct(one.shape, jnp.bfloat16),
        compiler_params=params(4),
        name="add_after",
    )(one, other, after)


def hold(value, after):
    anywhere = pl.BlockSpec(memory_space=pl.ANY)

    def kernel(value_ref, after_ref, out_ref):
        pass

    return pl.pallas_call(
        kernel,
        in_specs=[anywhere, anywhere],
        out_specs=anywhere,
        out_shape=jax.ShapeDtypeStruct(value.shape, value.dtype),
        input_output_aliases={0: 0},
        compiler_params=params(4),
        name="hold",
    )(value, after)


def local(
    dense_feats, lookup_ids, lookup_counts, shard_table, embed_tables, first_layer, first_offset, second_layer,
    second_offset, third_layer, third_offset, cross_down, cross_up, cross_bias, cotangent,
):
    examples = dense_feats.shape[0]
    devices = lookup_ids.shape[2] // examples
    weights = lax.all_gather(jnp.concatenate([cross_up, cross_down.T], axis=1), TABLE, axis=0, tiled=True)
    hits, pooled = pool(lookup_ids, lookup_counts, embed_tables)
    pooled = pooled.reshape(devices, examples, pooled.shape[1])
    arrived = lax.all_to_all(pooled, TABLE, split_axis=0, concat_axis=0, tiled=True)
    vmem = pl.BlockSpec(memory_space=pltpu.VMEM)
    bottom_args = (
        dense_feats, first_layer, first_offset[None], second_layer, second_offset[None], third_layer,
        third_offset[None],
    )
    bottom_out = pl.pallas_call(
        bottom_kernel,
        in_specs=[vmem] * 7,
        out_specs=vmem,
        out_shape=jax.ShapeDtypeStruct((examples, WIDTH), jnp.bfloat16),
        compiler_params=params(8),
        name="bottom",
    )(*bottom_args)
    send, bottom_grad, bias_part = cross(shard_table, arrived, bottom_out, weights, cross_bias[None], cotangent)
    returned = lax.all_to_all(send, TABLE, split_axis=0, concat_axis=0, tiled=True)
    parts = lax.axis_size(DP)
    packed = pl.pallas_call(
        bottom_back_kernel,
        in_specs=[vmem] * 9,
        out_specs=vmem,
        out_shape=jax.ShapeDtypeStruct((8 * CHUNK, 128), jnp.bfloat16),
        compiler_params=params(8),
        name="bottom_back",
    )(*bottom_args, bottom_grad, bias_part)
    core, column = lax.axis_index("c"), lax.axis_index("x")
    length = lax.axis_size("x")
    packed = packed.reshape(length, 2, CHUNK, 128)
    theirs = lax.dynamic_index_in_dim(packed, 1 - core, axis=1, keepdims=False)
    came = lax.ppermute(theirs, "c", [(0, 1), (1, 0)])
    mine = lax.dynamic_index_in_dim(packed, core, axis=1, keepdims=False)
    both = mine.astype(jnp.float32) + came.astype(jnp.float32)
    part = lax.dynamic_index_in_dim(both, column, axis=0, keepdims=False)
    narrow = both.astype(jnp.bfloat16)
    for shift in range(1, length):
        piece = lax.dynamic_index_in_dim(narrow, (column + shift) % length, axis=0, keepdims=False)
        piece = lax.ppermute(piece, "x", [(place, (place + shift) % length) for place in range(length)])
        part = part + piece.astype(jnp.float32)
    part = spread_sum(part, "zl", (1,), returned)
    group = ("zh", "yl")
    part = jnp.broadcast_to(part.astype(jnp.bfloat16), (lax.axis_size(group), CHUNK, 128))
    part = lax.all_to_all(part, group, split_axis=0, concat_axis=0, tiled=True)
    part = jnp.sum(part.astype(jnp.float32), axis=0)

    table_parts = table_grads(hits, returned.reshape(-1, returned.shape[2]), parts)
    table_parts = hold(table_parts, part)
    table_parts = lax.all_to_all(table_parts, DP, split_axis=0, concat_axis=0, tiled=True)
    table_grad = jnp.sum(table_parts.astype(jnp.float32), axis=0)

    sent = part.astype(jnp.bfloat16)
    four = [
        lax.ppermute(sent, "yh", [(place, place ^ distance) for place in range(4)]).astype(jnp.float32)
        for distance in (1, 2, 3)
    ]
    part = ((sent.astype(jnp.float32) + four[0]) + (four[1] + four[2])).astype(jnp.bfloat16)
    other = lax.ppermute(part, "c", [(0, 1), (1, 0)])
    pair = jnp.where(core == 0, jnp.stack([part, other]), jnp.stack([other, part]))
    whole = lax.all_gather(pair.reshape(2 * CHUNK, 128), "x", axis=0, tiled=True)
    first_grad, second_grad, third_grad, first_sum, second_sum, third_sum, bias_sum = pl.pallas_call(
        unpack_kernel,
        in_specs=[vmem],
        out_specs=[vmem] * 7,
        out_shape=[
            jax.ShapeDtypeStruct(shape, jnp.float32)
            for shape in (
                first_layer.shape, second_layer.shape, third_layer.shape, (1, first_layer.shape[1]),
                (1, second_layer.shape[1]), (1, third_layer.shape[1]), (1, cross_bias.shape[0]),
            )
        ],
        compiler_params=params(8),
        name="unpack",
    )(whole)
    return (
        table_grad, first_grad, first_sum[0], second_grad, second_sum[0], third_grad, third_sum[0], bias_sum[0],
    )


def solution(mesh):
    fine = Mesh(mesh.devices.reshape(4, 4, 2, 4, 2, 2), EVERY)
    placed = (
        P(EVERY, None),
        P(TABLE, None, DP),
        P(TABLE, DP),
        P(),
        P(TABLE, None, None),
        P(),
        P(),
        P(),
        P(),
        P(),
        P(),
        P(None, TABLE),
        P(TABLE, None),
        P(),
        P(EVERY, None),
    )
    return jax.shard_map(
        local,
        mesh=fine,
        in_specs=placed,
        out_specs=(P(TABLE, DP, None), P(), P(), P(), P(), P(), P(), P()),
        check_vma=False,
    )
```

```python
import math

import jax
import jax.numpy as jnp
from jax import lax
from jax.experimental import pallas as pl
from jax.experimental.pallas import tpu as pltpu
from jax.sharding import Mesh
from jax.sharding import PartitionSpec as P

TABLES = 26
WIDTH = 128
GROUP = 32
BLOCK = 512
LOW = 256
TABLE = ("yh", "yl", "c")
DP = ("x", "zh", "zl")
EVERY = ("x", "zh", "zl", "yh", "yl", "c")
CHUNK = 176

NT = (((1,), (1,)), ((), ()))
TN = (((0,), (0,)), ((), ()))


def dot(a, b, dims=(((1,), (0,)), ((), ()))):
    return lax.dot_general(a, b, dims, preferred_element_type=jnp.float32)


def params(megabytes):
    return pltpu.CompilerParams(vmem_limit_bytes=megabytes * 1024 * 1024)


def pool_kernel(code_ref, table_ref, hits_ref, pooled_ref):
    slots = code_ref.shape[2]
    rows = table_ref.shape[1]
    lane = lax.broadcasted_iota(jnp.int32, (GROUP, slots), 1)
    own = (lane & (GROUP - 1)) == lax.broadcasted_iota(jnp.int32, (GROUP, slots), 0)
    low_iota = lax.broadcasted_iota(jnp.int32, (LOW, slots), 0).astype(jnp.float32).astype(jnp.bfloat16)
    one = jnp.ones((), jnp.bfloat16)
    zero = jnp.zeros((), jnp.bfloat16)
    for group in range(BLOCK // GROUP):
        code = code_ref[0, pl.ds(group, 1), :]
        high = jnp.broadcast_to(code >> 8, (GROUP, slots))
        high = jnp.where(own, high, -1).astype(jnp.float32).astype(jnp.bfloat16)
        low = (code & (LOW - 1)).astype(jnp.float32).astype(jnp.bfloat16)
        right = jnp.where(low_iota == jnp.broadcast_to(low, (LOW, slots)), one, zero)
        left = jnp.concatenate(
            [jnp.where(high == jnp.full((), part, jnp.bfloat16), one, zero) for part in range(rows // LOW)], axis=0
        )
        hits = dot(left, right, NT).astype(jnp.bfloat16)
        for part in range(rows // LOW):
            hits_ref[0, part, pl.ds(group * GROUP, GROUP), :] = hits[part * GROUP : (part + 1) * GROUP]
    total = dot(hits_ref[0, 0], table_ref[0, 0:LOW])
    for part in range(1, rows // LOW):
        total = total + dot(hits_ref[0, part], table_ref[0, part * LOW : part * LOW + LOW])
    pooled_ref[...] = total.astype(jnp.bfloat16)


def pool(lookup_ids, lookup_counts, embed_tables):
    shards, hot, batch = lookup_ids.shape
    rows = embed_tables.shape[1]
    slot = lax.broadcasted_iota(jnp.int32, lookup_ids.shape, 1)
    code = jnp.where(lookup_counts[:, None, :] > slot, lookup_ids, -1)
    code = code.reshape(shards, hot, batch // GROUP, GROUP).transpose(0, 2, 1, 3)
    code = code.reshape(shards, batch // GROUP, hot * GROUP)
    return pl.pallas_call(
        pool_kernel,
        grid=(shards, batch // BLOCK),
        in_specs=[
            pl.BlockSpec((1, BLOCK // GROUP, hot * GROUP), lambda s, b: (s, b, 0)),
            pl.BlockSpec((1, rows, WIDTH), lambda s, b: (s, 0, 0)),
        ],
        out_specs=[
            pl.BlockSpec((1, rows // LOW, BLOCK, LOW), lambda s, b: (s, 0, b, 0)),
            pl.BlockSpec((BLOCK, WIDTH), lambda s, b: (b, s)),
        ],
        out_shape=[
            pltpu.HBM((shards, rows // LOW, batch, LOW), jnp.bfloat16),
            jax.ShapeDtypeStruct((batch, shards * WIDTH), jnp.bfloat16),
        ],
        compiler_params=params(16),
        name="pool",
    )(code, embed_tables)


def table_grad_kernel(hits_ref, grad_ref, out_ref, turned):
    @pl.when(pl.program_id(1) == 0)
    def _():
        turned[...] = grad_ref[...].T

    blocks = hits_ref.shape[1]
    step = out_ref.shape[0] // blocks
    for block in range(blocks):
        total = dot(turned[...], hits_ref[0, block]).T.astype(jnp.bfloat16)
        out_ref[block * step : block * step + step] = total.reshape(step, *out_ref.shape[1:])


def table_grads(hits, grads, parts):
    shards, blocks, batch, low = hits.shape
    each = blocks * low // parts
    wide = math.gcd(blocks, 4)
    step = wide * low // each
    return pl.pallas_call(
        table_grad_kernel,
        grid=(shards, blocks // wide),
        in_specs=[
            pl.BlockSpec((1, wide, batch, low), lambda s, r: (s, r, 0, 0)),
            pl.BlockSpec((batch, WIDTH), lambda s, r: (0, s)),
        ],
        out_specs=pl.BlockSpec((step, 1, each, WIDTH), lambda s, r: (r, s, 0, 0)),
        out_shape=jax.ShapeDtypeStruct((parts, shards, each, WIDTH), jnp.bfloat16),
        scratch_shapes=[pltpu.VMEM((WIDTH, batch), jnp.bfloat16)],
        compiler_params=params(46),
        cost_estimate=pl.CostEstimate(
            flops=2 * shards * batch * blocks * low * WIDTH,
            bytes_accessed=2 * shards * batch * (blocks * low + 2 * WIDTH),
            transcendentals=0,
        ),
        name="table_grads",
    )(hits, grads)


def silu(value):
    return value / (1.0 + jnp.exp(-value))


def silu_slope(value):
    sigmoid = 1.0 / (1.0 + jnp.exp(-value))
    return sigmoid * (1.0 + value * (1.0 - sigmoid))


def bottom_pre(dense, w1, b1, w2, b2, w3, b3):
    first_pre = dot(dense[...], w1[...]) + b1[...]
    first_act = silu(first_pre).astype(jnp.bfloat16)
    second_pre = dot(first_act, w2[...]) + b2[...]
    second_act = silu(second_pre).astype(jnp.bfloat16)
    third_pre = dot(second_act, w3[...]) + b3[...]
    return first_pre, first_act, second_pre, second_act, third_pre


def bottom_kernel(dense, w1, b1, w2, b2, w3, b3, out_ref):
    out_ref[...] = silu(bottom_pre(dense, w1, b1, w2, b2, w3, b3)[4]).astype(jnp.bfloat16)


def bottom_back_kernel(dense, w1, b1, w2, b2, w3, b3, grad_ref, bias_ref, out_ref):
    first_pre, first_act, second_pre, second_act, third_pre = bottom_pre(dense, w1, b1, w2, b2, w3, b3)
    third_delta = silu_slope(third_pre) * grad_ref[...].astype(jnp.float32)
    third_delta = third_delta.astype(jnp.bfloat16)
    out_ref[1024:1280, :] = dot(second_act, third_delta, TN).astype(jnp.bfloat16)
    second_delta = (silu_slope(second_pre) * dot(third_delta, w3[...], NT)).astype(jnp.bfloat16)
    second_grad = dot(first_act, second_delta, TN).astype(jnp.bfloat16)
    out_ref[0:512, :] = second_grad[:, :128]
    out_ref[512:1024, :] = second_grad[:, 128:]
    first_delta = (silu_slope(first_pre) * dot(second_delta, w2[...], NT)).astype(jnp.bfloat16)
    first_grad = dot(dense[...], first_delta, TN)
    first_grad = jnp.concatenate([first_grad, jnp.zeros((3, first_grad.shape[1]), jnp.float32)], axis=0)
    for part in range(4):
        out_ref[1280 + 16 * part : 1296 + 16 * part, :] = first_grad[:, part * 128 : part * 128 + 128].astype(
            jnp.bfloat16
        )
    first_sum = jnp.sum(first_delta.astype(jnp.float32), axis=0, keepdims=True)
    second_sum = jnp.sum(second_delta.astype(jnp.float32), axis=0, keepdims=True)
    third_sum = jnp.sum(third_delta.astype(jnp.float32), axis=0, keepdims=True)
    rows = [first_sum[:, part * 128 : part * 128 + 128] for part in range(4)]
    rows += [second_sum[:, part * 128 : part * 128 + 128] for part in range(2)]
    rows += [third_sum, jnp.zeros((9, 128), jnp.float32)]
    out_ref[1344:1360, :] = jnp.concatenate(rows, axis=0).astype(jnp.bfloat16)
    out_ref[1360:1392, :] = bias_ref[...].astype(jnp.bfloat16)
    out_ref[1392:1408, :] = jnp.zeros((16, 128), jnp.bfloat16)


def unpack_kernel(whole, first_grad, second_grad, third_grad, first_sum, second_sum, third_sum, bias_sum):
    second_grad[:, 0:128] = whole[0:512].astype(jnp.float32)
    second_grad[:, 128:256] = whole[512:1024].astype(jnp.float32)
    third_grad[...] = whole[1024:1280].astype(jnp.float32)
    for part in range(4):
        block = whole[1280 + 16 * part : 1296 + 16 * part].astype(jnp.float32)
        first_grad[:, part * 128 : part * 128 + 128] = block[0:13]
    sums = whole[1344:1360].astype(jnp.float32)
    for part in range(4):
        first_sum[:, part * 128 : part * 128 + 128] = sums[part : part + 1]
    for part in range(2):
        second_sum[:, part * 128 : part * 128 + 128] = sums[4 + part : 5 + part]
    third_sum[...] = sums[6:7]
    biases = whole[1360:1392].astype(jnp.float32)
    for part in range(27):
        bias_sum[:, part * 128 : part * 128 + 128] = biases[part : part + 1]


def cross_kernel(
    owner_ref, arrived_ref, bottom_ref, weights_ref, bias_ref, cot_ref,
    send_ref, bottom_grad_ref, bias_grad_ref, total, inputs, mixed, grads, up, down, arrived_at,
):
    blocks = total.shape[0]
    wide = blocks * WIDTH
    shards = owner_ref.shape[0]
    fetch_down = pltpu.make_async_copy(weights_ref.at[:, wide : 2 * wide], down, arrived_at.at[0])
    fetch_up = pltpu.make_async_copy(weights_ref.at[:, 0:wide], up, arrived_at.at[1])
    fetch_down.start()
    fetch_up.start()
    total[1:] = jnp.zeros_like(total[1:])
    total[0] = bottom_ref[...].astype(jnp.float32)
    for shard in range(shards):
        place = owner_ref[shard] + 1
        piece = arrived_ref[shard // 2, :, (shard % 2) * WIDTH : (shard % 2) * WIDTH + WIDTH]
        total[place] = total[place] + piece.astype(jnp.float32)
    bias_grad_ref[...] = jnp.zeros_like(bias_grad_ref)
    for block in range(blocks):
        columns = slice(block * WIDTH, block * WIDTH + WIDTH)
        piece = total[block].astype(jnp.bfloat16)
        inputs[:, columns] = piece
        mix_grad = cot_ref[:, columns].astype(jnp.float32) * piece.astype(jnp.float32)
        mixed[:, columns] = mix_grad.astype(jnp.bfloat16)
        bias_grad_ref[block : block + 1, :] = jnp.sum(mix_grad, axis=0, keepdims=True)
    fetch_down.wait()
    low_rank = dot(inputs[...], down[...], NT).astype(jnp.bfloat16)
    fetch_up.wait()
    rank_grad = dot(mixed[...], up[...], NT).astype(jnp.bfloat16)
    step = 3 * WIDTH
    for part in range(wide // step):
        columns = slice(part * step, part * step + step)
        mixing = dot(low_rank, up[:, columns]) + bias_ref[:, columns]
        back = dot(rank_grad, down[:, columns])
        grad = (cot_ref[:, columns].astype(jnp.float32) * (mixing + 1.0) + back).astype(jnp.bfloat16)
        for inner in range(3):
            grads[part * 3 + inner] = grad[:, inner * WIDTH : inner * WIDTH + WIDTH]
    bottom_grad_ref[...] = grads[0]
    for shard in range(shards):
        send_ref[shard // 2, :, (shard % 2) * WIDTH : (shard % 2) * WIDTH + WIDTH] = grads[owner_ref[shard] + 1]


def cross(shard_table, arrived, bottom_out, weights, cross_bias, cotangent):
    examples, wide = cotangent.shape
    blocks = wide // WIDTH
    vmem = pl.BlockSpec(memory_space=pltpu.VMEM)
    return pl.pallas_call(
        cross_kernel,
        in_specs=[pl.BlockSpec(memory_space=pltpu.SMEM), vmem, vmem, pl.BlockSpec(memory_space=pltpu.HBM), vmem, vmem],
        out_specs=[vmem] * 3,
        out_shape=[
            jax.ShapeDtypeStruct(arrived.shape, jnp.bfloat16),
            jax.ShapeDtypeStruct((examples, WIDTH), jnp.bfloat16),
            jax.ShapeDtypeStruct((32, WIDTH), jnp.float32),
        ],
        scratch_shapes=[
            pltpu.VMEM((blocks, examples, WIDTH), jnp.float32),
            pltpu.VMEM((examples, wide), jnp.bfloat16),
            pltpu.VMEM((examples, wide), jnp.bfloat16),
            pltpu.VMEM((blocks, examples, WIDTH), jnp.bfloat16),
            pltpu.VMEM((weights.shape[0], wide), jnp.bfloat16),
            pltpu.VMEM((weights.shape[0], wide), jnp.bfloat16),
            pltpu.SemaphoreType.DMA((2,)),
        ],
        compiler_params=params(55),
        name="cross",
    )(shard_table, arrived, bottom_out, weights, cross_bias, cotangent)


def spread_sum(value, axis, distances, after=None):
    size = lax.axis_size(axis)
    for distance in distances:
        sent = value.astype(jnp.bfloat16)
        came = lax.ppermute(sent, axis, [(place, place ^ distance) for place in range(size)])
        if after is None:
            value = sent.astype(jnp.float32) + came.astype(jnp.float32)
        else:
            value = add_after(sent, came, after)
    return value


def add_kernel(one_ref, other_ref, after_ref, out_ref):
    out_ref[...] = (one_ref[...].astype(jnp.float32) + other_ref[...].astype(jnp.float32)).astype(jnp.bfloat16)


def add_after(one, other, after):
    vmem = pl.BlockSpec(memory_space=pltpu.VMEM)
    return pl.pallas_call(
        add_kernel,
        in_specs=[vmem, vmem, pl.BlockSpec(memory_space=pl.ANY)],
        out_specs=vmem,
        out_shape=jax.ShapeDtypeStruct(one.shape, jnp.bfloat16),
        compiler_params=params(4),
        name="add_after",
    )(one, other, after)


def hold(value, after):
    anywhere = pl.BlockSpec(memory_space=pl.ANY)

    def kernel(value_ref, after_ref, out_ref):
        pass

    return pl.pallas_call(
        kernel,
        in_specs=[anywhere, anywhere],
        out_specs=anywhere,
        out_shape=jax.ShapeDtypeStruct(value.shape, value.dtype),
        input_output_aliases={0: 0},
        compiler_params=params(4),
        name="hold",
    )(value, after)


def local(
    dense_feats, lookup_ids, lookup_counts, shard_table, embed_tables, first_layer, first_offset, second_layer,
    second_offset, third_layer, third_offset, cross_down, cross_up, cross_bias, cotangent,
):
    examples = dense_feats.shape[0]
    devices = lookup_ids.shape[2] // examples
    weights = lax.all_gather(jnp.concatenate([cross_up, cross_down.T], axis=1), TABLE, axis=0, tiled=True)
    hits, pooled = pool(lookup_ids, lookup_counts, embed_tables)
    pooled = pooled.reshape(devices, examples, pooled.shape[1])
    arrived = lax.all_to_all(pooled, TABLE, split_axis=0, concat_axis=0, tiled=True)
    vmem = pl.BlockSpec(memory_space=pltpu.VMEM)
    bottom_args = (
        dense_feats, first_layer, first_offset[None], second_layer, second_offset[None], third_layer,
        third_offset[None],
    )
    bottom_out = pl.pallas_call(
        bottom_kernel,
        in_specs=[vmem] * 7,
        out_specs=vmem,
        out_shape=jax.ShapeDtypeStruct((examples, WIDTH), jnp.bfloat16),
        compiler_params=params(8),
        name="bottom",
    )(*bottom_args)
    send, bottom_grad, bias_part = cross(shard_table, arrived, bottom_out, weights, cross_bias[None], cotangent)
    returned = lax.all_to_all(send, TABLE, split_axis=0, concat_axis=0, tiled=True)
    parts = lax.axis_size(DP)
    packed = pl.pallas_call(
        bottom_back_kernel,
        in_specs=[vmem] * 9,
        out_specs=vmem,
        out_shape=jax.ShapeDtypeStruct((8 * CHUNK, 128), jnp.bfloat16),
        compiler_params=params(8),
        name="bottom_back",
    )(*bottom_args, bottom_grad, bias_part)
    core, column = lax.axis_index("c"), lax.axis_index("x")
    length = lax.axis_size("x")
    packed = packed.reshape(length, 2, CHUNK, 128)
    theirs = lax.dynamic_index_in_dim(packed, 1 - core, axis=1, keepdims=False)
    came = lax.ppermute(theirs, "c", [(0, 1), (1, 0)])
    mine = lax.dynamic_index_in_dim(packed, core, axis=1, keepdims=False)
    both = mine.astype(jnp.float32) + came.astype(jnp.float32)
    part = lax.dynamic_index_in_dim(both, column, axis=0, keepdims=False)
    narrow = both.astype(jnp.bfloat16)
    for shift in range(1, length):
        piece = lax.dynamic_index_in_dim(narrow, (column + shift) % length, axis=0, keepdims=False)
        piece = lax.ppermute(piece, "x", [(place, (place + shift) % length) for place in range(length)])
        part = part + piece.astype(jnp.float32)
    part = spread_sum(part, "zl", (1,), returned)
    group = ("zh", "yl")
    part = jnp.broadcast_to(part.astype(jnp.bfloat16), (lax.axis_size(group), CHUNK, 128))
    part = lax.all_to_all(part, group, split_axis=0, concat_axis=0, tiled=True)
    part = jnp.sum(part.astype(jnp.float32), axis=0)

    table_parts = table_grads(hits, returned.reshape(-1, returned.shape[2]), parts)
    table_parts = hold(table_parts, part)
    table_parts = lax.all_to_all(table_parts, DP, split_axis=0, concat_axis=0, tiled=True)
    table_grad = jnp.sum(table_parts.astype(jnp.float32), axis=0)

    sent = part.astype(jnp.bfloat16)
    four = [
        lax.ppermute(sent, "yh", [(place, place ^ distance) for place in range(4)]).astype(jnp.float32)
        for distance in (1, 2, 3)
    ]
    part = ((sent.astype(jnp.float32) + four[0]) + (four[1] + four[2])).astype(jnp.bfloat16)
    other = lax.ppermute(part, "c", [(0, 1), (1, 0)])
    pair = jnp.where(core == 0, jnp.stack([part, other]), jnp.stack([other, part]))
    whole = lax.all_gather(pair.reshape(2 * CHUNK, 128), "x", axis=0, tiled=True)
    first_grad, second_grad, third_grad, first_sum, second_sum, third_sum, bias_sum = pl.pallas_call(
        unpack_kernel,
        in_specs=[vmem],
        out_specs=[vmem] * 7,
        out_shape=[
            jax.ShapeDtypeStruct(shape, jnp.float32)
            for shape in (
                first_layer.shape, second_layer.shape, third_layer.shape, (1, first_layer.shape[1]),
                (1, second_layer.shape[1]), (1, third_layer.shape[1]), (1, cross_bias.shape[0]),
            )
        ],
        compiler_params=params(8),
        name="unpack",
    )(whole)
    return (
        table_grad, first_grad, first_sum[0], second_grad, second_sum[0], third_grad, third_sum[0], bias_sum[0],
    )


def solution(mesh):
    fine = Mesh(mesh.devices.reshape(4, 4, 2, 4, 2, 2), EVERY)
    placed = (
        P(EVERY, None),
        P(TABLE, None, DP),
        P(TABLE, DP),
        P(),
        P(TABLE, None, None),
        P(),
        P(),
        P(),
        P(),
        P(),
        P(),
        P(None, TABLE),
        P(TABLE, None),
        P(),
        P(EVERY, None),
    )
    return jax.shard_map(
        local,
        mesh=fine,
        in_specs=placed,
        out_specs=(P(TABLE, DP, None), P(), P(), P(), P(), P(), P(), P()),
        check_vma=False,
    )
```
